32 devices in a mesh: copies: 2 (over y), fsdp: 4 (over z), adapter: 4 (over x, core).
Axes of the slice: x: 2, y: 2, z: 4, core: 2. Of those that a mesh axis runs over, the one named last changes fastest.
Arguments:
- tokens: bfloat16 [8192, 5120], P(('copies', 'fsdp', 'adapter')), parts along dimension 0, may hold values from -6 to 6
- frozen_key_weight: bfloat16 [5120, 1024], P('fsdp'), may hold values from -0.078125 to 0.078125
- key_norm_gain: float32 [128], replicated, may hold values from 0.5 to 1.5
- adapter_down_weight: bfloat16 [48, 64, 5120], P('adapter', None, 'fsdp'), may hold values from -0.078125 to 0.078125
- adapter_up_weight: bfloat16 [48, 64, 1024], P('adapter', None, 'fsdp'), may hold values from -0.75 to 0.75
- packed_block_adapter: int32 [32], P('copies'), parts along dimension 0, may hold values from 0 to 47, as said below
- adapter_storage_row: int32 [48], replicated, may hold values from 0 to 47, each once
- live_adapter_rank: int32 [48], replicated, may hold values from 8 to 64, as said below
- document_numbers: int32 [8192], P(('copies', 'fsdp', 'adapter')), parts along dimension 0, may hold values from 0 to 4095, as said below
- rotated_key_gradient: bfloat16 [8192, 1024], P(('copies', 'fsdp', 'adapter')), parts along dimension 0, may hold values from -0.119628906 to 0.119628906
Outputs:
- rotated_keys: bfloat16 [8192, 1024], P(('copies', 'fsdp', 'adapter')), parts along dimension 0
- grad_down: float32 [96, 64, 5120], P(('copies', 'adapter'), None, 'fsdp'), parts along dimension 0
- grad_up: float32 [96, 64, 1024], P(('copies', 'adapter'), None, 'fsdp'), parts along dimension 0
The draws below stay inside these ranges and needn't reach their ends.
There are 2 independent parts, one for each index of `copies`. The reference program is written for one: setup_inputs(seed, part) draws one part's arguments, and reference() takes and returns one part's arrays. A program takes and returns all parts, laid end to end along the dimension named above; an argument that names none is the same for every part. Nothing has to cross between parts.
Inputs may be any that keep to these rules, and one draw needn't show every extreme that they name: `packed_block_adapter`: never falling along the blocks; block 0 names adapter 0 and the last block names adapter 48 - 1. `live_adapter_rank`: each is 64 divided by 1, 2, 4 or 8; both ends are taken. `document_numbers`: never falling; a new document starts at every multiple of 256, so no document crosses a block; each id is the index of its document's first token, and the last token is a document of its own.
All inputs are finite; a program needn't handle non-finite values.
Results may differ from the reference program's by a relative error of at most 0.007.
Values may be sent and summed in bfloat16 or wider, within the bound.
No kernel may reach another device: no remote copies, remote signals or barrier semaphores. Data moves between devices by JAX's collectives and lax.ppermute only.
A program may use at most 128 MiB of HBM per device.

```python
import jax
import jax.numpy as jnp
from jax import lax

MODEL_WIDTH = 5120
HEAD = 128
PADDED_RANK = 64
ADAPTER_COUNT = 48
BLOCK_LENGTH = 256
KEY_FEATURES = 1024
NBLOCKS = 16
TOKENS = 4096


def draw_packed_block_adapter(key, part):
    key = jax.random.fold_in(key, 11)
    key_one, key_two = jax.random.split(key)
    first_draw = jax.random.randint(key_one, (NBLOCKS,), 0, ADAPTER_COUNT)
    second_draw = jax.random.randint(key_two, (NBLOCKS,), 1, ADAPTER_COUNT + 1)
    chosen = jnp.sort(first_draw * second_draw // ADAPTER_COUNT)
    chosen = chosen.at[0].set(0).at[NBLOCKS - 1].set(ADAPTER_COUNT - 1)
    return chosen.astype(jnp.int32)


def draw_live_adapter_rank(key, part):
    key = jax.random.fold_in(key, 12)
    shifts = jax.random.randint(key, (ADAPTER_COUNT,), 0, 4)
    ranks = PADDED_RANK // jnp.left_shift(jnp.ones((ADAPTER_COUNT,), jnp.int32), shifts)
    ranks = ranks.at[0].set(PADDED_RANK).at[1].set(PADDED_RANK // 8)
    return ranks.astype(jnp.int32)


def draw_document_numbers(key, part):
    key = jax.random.fold_in(key, 13)
    rolls = jax.random.randint(key, (TOKENS,), 0, 24)
    index_iota = jnp.arange(TOKENS, dtype=jnp.int32)
    starts = jnp.logical_or(rolls == 0, index_iota % BLOCK_LENGTH == 0)
    starts = jnp.logical_or(starts, index_iota == TOKENS - 1)
    first_index = lax.cummax(jnp.where(starts, index_iota, 0), axis=0)
    return first_index.astype(jnp.int32)


def shard_levels(key, dims, cuts, least, high):
    def one(dim, blocks):
        steps = jax.random.uniform(jax.random.fold_in(jax.random.fold_in(key, 6), dim), (blocks,), jnp.float32, least / len(cuts), high / len(cuts))
        return jnp.repeat(jnp.exp(steps), dims[dim] // blocks).reshape((-1,) + (1,) * (len(dims) - dim - 1))

    factor_of = one(*cuts[0])
    for cut in cuts[1:]:
        factor_of = factor_of * one(*cut)
    return factor_of


def scatter_about(key, dims, scale, most, shards=(), held_as=jnp.bfloat16):
    gain = shard_levels(key, dims, shards, -0.22, 0.18) if shards else 1.0
    entries = jax.random.normal(key, dims, jnp.float32) * scale * gain
    return jnp.minimum(jnp.maximum(entries, -most), most).astype(held_as)


def setup_inputs(seed: int = 0, part: int = 0) -> dict:
    seeds = jax.random.split(jax.random.key(seed), 11)
    own_keys = jax.random.split(jax.random.fold_in(seeds[10], part), 11)
    tokens = scatter_about(own_keys[0], (TOKENS, MODEL_WIDTH), 1.0, 6.0, ((0, 16),))
    frozen_key_weight = scatter_about(seeds[1], (MODEL_WIDTH, KEY_FEATURES), MODEL_WIDTH ** -0.5, 0.078125, ((0, 4),))
    key_norm_gain = jnp.clip(1.0 + 0.1 * jax.random.normal(seeds[2], (HEAD,), jnp.float32), 0.5, 1.5)
    adapter_down_weight = scatter_about(seeds[3], (ADAPTER_COUNT, PADDED_RANK, MODEL_WIDTH), MODEL_WIDTH ** -0.5, 0.078125, ((0, 4), (2, 4)))
    adapter_up_weight = scatter_about(seeds[4], (ADAPTER_COUNT, PADDED_RANK, KEY_FEATURES), PADDED_RANK ** -0.5, 0.75, ((0, 4), (2, 4)))
    packed_block_adapter = draw_packed_block_adapter(jax.random.fold_in(jax.random.fold_in(seeds[10], part), 71), part)
    adapter_storage_row = jax.random.permutation(seeds[6], ADAPTER_COUNT).astype(jnp.int32)
    live_adapter_rank = draw_live_adapter_rank(jax.random.fold_in(seeds[10], 71), part)
    document_numbers = draw_document_numbers(jax.random.fold_in(jax.random.fold_in(seeds[10], part), 71), part)
    rotated_key_gradient = scatter_about(own_keys[9], (TOKENS, KEY_FEATURES), 0.02, 0.119628906, ((0, 16),))
    return {"tokens": tokens, "frozen_key_weight": frozen_key_weight, "key_norm_gain": key_norm_gain, "adapter_down_weight": adapter_down_weight, "adapter_up_weight": adapter_up_weight, "packed_block_adapter": packed_block_adapter, "adapter_storage_row": adapter_storage_row, "live_adapter_rank": live_adapter_rank, "document_numbers": document_numbers, "rotated_key_gradient": rotated_key_gradient}


ADAPTER_STRENGTH = 16.0
ROPE_BASE = 1000000.0

def rope_tables(positions, head_size):
    half_head = head_size // 2
    steps_iota = jnp.arange(half_head, dtype=jnp.float32)
    frequency = jnp.exp(-jnp.log(jnp.float32(ROPE_BASE)) * 2.0 * steps_iota / head_size)
    angles = positions.astype(jnp.float32)[:, None] * frequency[None, :]
    return (jnp.cos(angles), jnp.sin(angles))

def keys_from(before_norm_keys, cosine_part, sine_part, key_norm_gain):
    rows_count = before_norm_keys.shape[0]
    head_size = key_norm_gain.shape[0]
    half_head = head_size // 2
    heads = before_norm_keys.reshape(rows_count, -1, head_size)
    mean_square = lax.optimization_barrier(jnp.mean(heads * heads, axis=-1, keepdims=True))
    normed = heads * lax.rsqrt(mean_square + 1e-06) * key_norm_gain
    first_half = normed[..., :half_head]
    second_half = normed[..., half_head:]
    cosine_wide = cosine_part[:, None, :]
    sine_wide = sine_part[:, None, :]
    turned = jnp.concatenate([first_half * cosine_wide - second_half * sine_wide, second_half * cosine_wide + first_half * sine_wide], axis=-1)
    return turned.reshape(rows_count, -1)

def doc_positions(document_numbers):
    count = document_numbers.shape[0]
    index_iota = jnp.arange(count, dtype=jnp.int32)
    previous = jnp.concatenate([document_numbers[:1], document_numbers[:-1]])
    doc_start = jnp.logical_or(index_iota % BLOCK_LENGTH == 0, document_numbers != previous)
    first_index = lax.cummax(jnp.where(doc_start, index_iota, 0), axis=0)
    return index_iota - first_index

def reference(tokens, frozen_key_weight, key_norm_gain, adapter_down_weight, adapter_up_weight, packed_block_adapter, adapter_storage_row, live_adapter_rank, document_numbers, rotated_key_gradient):
    positions = doc_positions(document_numbers)
    cosine_all, sine_all = rope_tables(positions, HEAD)
    half_head = HEAD // 2
    block_items = (tokens.reshape(NBLOCKS, BLOCK_LENGTH, MODEL_WIDTH), rotated_key_gradient.reshape(NBLOCKS, BLOCK_LENGTH, KEY_FEATURES), cosine_all.reshape(NBLOCKS, BLOCK_LENGTH, half_head), sine_all.reshape(NBLOCKS, BLOCK_LENGTH, half_head), packed_block_adapter)

    def block_step(totals, block_item):
        block_tokens, block_grad, cosine_part, sine_part, adapter_id = block_item
        storage_row_index = adapter_storage_row[adapter_id]
        current_rank = live_adapter_rank[adapter_id]
        down_weight_table = adapter_down_weight[storage_row_index]
        up_weight_table = adapter_up_weight[storage_row_index]
        rank_mask = (jnp.arange(PADDED_RANK, dtype=jnp.int32) < current_rank).astype(jnp.float32)
        adapter_scale = ADAPTER_STRENGTH / current_rank.astype(jnp.float32)
        frozen_portion = jnp.dot(block_tokens, frozen_key_weight, preferred_element_type=jnp.float32)
        reduced_rank_state = (jnp.dot(block_tokens, down_weight_table.T, preferred_element_type=jnp.float32) * rank_mask).astype(jnp.bfloat16)
        adapter_update = jnp.dot(reduced_rank_state, up_weight_table, preferred_element_type=jnp.float32)
        before_norm_keys = frozen_portion + adapter_scale * adapter_update

        def rotate(values):
            return keys_from(values, cosine_part, sine_part, key_norm_gain)
        rotated, pullback = jax.vjp(rotate, before_norm_keys)
        pre_norm_gradient = pullback(block_grad.astype(jnp.float32))[0]
        scaled_update = (adapter_scale * pre_norm_gradient).astype(jnp.bfloat16)
        grad_low = (jnp.dot(scaled_update, up_weight_table.T, preferred_element_type=jnp.float32) * rank_mask).astype(jnp.bfloat16)
        part_up = jnp.dot(reduced_rank_state.T, scaled_update, preferred_element_type=jnp.float32)
        part_down = jnp.dot(grad_low.T, block_tokens, preferred_element_type=jnp.float32)
        down_total, up_total = totals
        down_total = down_total.at[storage_row_index].add(part_down)
        up_total = up_total.at[storage_row_index].add(part_up)
        return ((down_total, up_total), rotated.astype(jnp.bfloat16))
    start_totals = (jnp.zeros((ADAPTER_COUNT, PADDED_RANK, MODEL_WIDTH), jnp.float32), jnp.zeros((ADAPTER_COUNT, PADDED_RANK, KEY_FEATURES), jnp.float32))
    (grad_down, grad_up), rotated_blocks = lax.scan(block_step, start_totals, block_items)
    return (rotated_blocks.reshape(TOKENS, KEY_FEATURES), grad_down, grad_up)
```

```python
import functools

import jax
import jax.numpy as jnp
from jax import lax
from jax.experimental import pallas as pl
from jax.experimental.pallas import tpu as pltpu
from jax.sharding import PartitionSpec as P

BLOCK_LENGTH = 256
ADAPTER_STRENGTH = 16.0
ROPE_BASE = 1000000.0


def rope_tables(positions, head_size):
    half_head = head_size // 2
    steps_iota = jnp.arange(half_head, dtype=jnp.float32)
    frequency = jnp.exp(-jnp.log(jnp.float32(ROPE_BASE)) * 2.0 * steps_iota / head_size)
    angles = positions.astype(jnp.float32)[:, None] * frequency[None, :]
    return (jnp.cos(angles), jnp.sin(angles))


def keys_from(before_norm_keys, cosine_part, sine_part, key_norm_gain):
    rows_count = before_norm_keys.shape[0]
    head_size = key_norm_gain.shape[0]
    half_head = head_size // 2
    heads = before_norm_keys.reshape(rows_count, -1, head_size)
    mean_square = jnp.mean(heads * heads, axis=-1, keepdims=True)
    normed = heads * lax.rsqrt(mean_square + 1e-06) * key_norm_gain
    first_half = normed[..., :half_head]
    second_half = normed[..., half_head:]
    cosine_wide = cosine_part[:, None, :]
    sine_wide = sine_part[:, None, :]
    turned = jnp.concatenate(
        [
            first_half * cosine_wide - second_half * sine_wide,
            second_half * cosine_wide + first_half * sine_wide,
        ],
        axis=-1,
    )
    return turned.reshape(rows_count, -1)


def doc_positions(document_numbers):
    count = document_numbers.shape[0]
    index_iota = jnp.arange(count, dtype=jnp.int32)
    previous = jnp.concatenate([document_numbers[:1], document_numbers[:-1]])
    doc_start = jnp.logical_or(index_iota % BLOCK_LENGTH == 0, document_numbers != previous)
    first_index = lax.cummax(jnp.where(doc_start, index_iota, 0), axis=0)
    return index_iota - first_index


def pick_kernel(own_rows, pair_rows, own_ref, pair_ref, out_ref):
    n = pl.program_id(0)
    own = own_rows[n] >= 0
    pair = pair_rows[n] >= 0
    out_ref[0] = jnp.zeros_like(out_ref[0])

    @pl.when(own)
    def _():
        out_ref[0] = own_ref[0]

    @pl.when(pair)
    def _():
        out_ref[0] = pair_ref[0]


def pick_rows(own, pair, own_rows, pair_rows):
    count = own_rows.shape[0]
    _, rank, width = own.shape
    return pl.pallas_call(
        pick_kernel,
        grid_spec=pltpu.PrefetchScalarGridSpec(
            num_scalar_prefetch=2,
            grid=(count,),
            in_specs=[
                pl.BlockSpec((1, rank, width), lambda n, o, p: (jnp.maximum(o[n], 0), 0, 0)),
                pl.BlockSpec((1, rank, width), lambda n, o, p: (jnp.maximum(p[n], 0), 0, 0)),
            ],
            out_specs=pl.BlockSpec((1, rank, width), lambda n, o, p: (n, 0, 0)),
        ),
        out_shape=jax.ShapeDtypeStruct((count, rank, width), own.dtype),
    )(own_rows, pair_rows, own, pair)


def owner_sum_kernel(arrays, per_array, owned, rows_ref, *refs):
    block_refs, down_ref, up_ref = refs[:arrays], refs[arrays], refs[arrays + 1]
    down_width = down_ref.shape[2]
    down_ref[...] = jnp.zeros_like(down_ref)
    up_ref[...] = jnp.zeros_like(up_ref)
    for i in range(arrays):

        def one(j, carry, i=i):
            row = rows_ref[i * per_array + j]

            @pl.when(jnp.logical_and(row >= 0, row < owned))
            def _():
                block = block_refs[i][j].astype(jnp.float32)
                down_ref[row] += block[:, :down_width]
                up_ref[row] += block[:, down_width:]

            return carry

        lax.fori_loop(0, per_array, one, 0)


def owner_sum(blocks, rows, owned, down_width):
    per_array, rank, width = blocks[0].shape
    tile = 16
    return pl.pallas_call(
        functools.partial(owner_sum_kernel, len(blocks), per_array, owned),
        grid_spec=pltpu.PrefetchScalarGridSpec(
            num_scalar_prefetch=1,
            grid=(rank // tile,),
            in_specs=[
                pl.BlockSpec((per_array, tile, width), lambda t, r: (0, t, 0)) for _ in blocks
            ],
            out_specs=[
                pl.BlockSpec((owned, tile, down_width), lambda t, r: (0, t, 0)),
                pl.BlockSpec((owned, tile, width - down_width), lambda t, r: (0, t, 0)),
            ],
        ),
        out_shape=[
            jax.ShapeDtypeStruct((owned, rank, down_width), jnp.float32),
            jax.ShapeDtypeStruct((owned, rank, width - down_width), jnp.float32),
        ],
        compiler_params=pltpu.CompilerParams(vmem_limit_bytes=40 * 1024 * 1024),
    )(rows, *blocks)


def per_device(
    tokens,
    frozen_key_weight,
    key_norm_gain,
    adapter_down_weight,
    adapter_up_weight,
    packed_block_adapter,
    adapter_storage_row,
    live_adapter_rank,
    document_numbers,
    rotated_key_gradient,
):
    rows = tokens.shape[0]
    features = rotated_key_gradient.shape[1]
    depth = frozen_key_weight.shape[0]
    owned, rank, down_width = adapter_down_weight.shape
    up_width = adapter_up_weight.shape[2]
    copies_n = lax.axis_size("copies")
    z_n = lax.axis_size("fsdp")
    group_n = lax.axis_size("adapter")
    x_n = group_n // 2
    y = lax.axis_index("copies")
    z = lax.axis_index("fsdp")
    a = lax.axis_index("adapter")
    x, core = a // 2, a % 2

    def over_core(v):
        return lax.ppermute(v, "adapter", [(i, i ^ 1) for i in range(group_n)])

    def over_x(v, e):
        return lax.ppermute(
            v, "adapter", [(i, ((i // 2 + e) % x_n) * 2 + i % 2) for i in range(group_n)]
        )

    def over_y(v, g):
        return lax.ppermute(v, "copies", [(i, (i + g) % copies_n) for i in range(copies_n)])

    def over_z(v, d):
        return lax.ppermute(v, "fsdp", [(i, (i + d) % z_n) for i in range(z_n)])

    half = features // 2
    units = copies_n * x_n
    unit_width = half // units
    unit = lax.dynamic_slice(
        frozen_key_weight,
        (0, core * half + (y * x_n + x) * unit_width),
        (depth, unit_width),
    )
    own_half = lax.dynamic_slice(frozen_key_weight, (0, core * half), (depth, half))
    from_z = {d: over_z(unit, d) for d in range(1, z_n)}
    tokens_pair = over_core(tokens)

    tables = jnp.concatenate([adapter_down_weight, adapter_up_weight], axis=2)
    tables_pair = over_core(tables)
    block_rows = adapter_storage_row[packed_block_adapter].reshape(z_n, x_n, 2)
    z_order = (z + jnp.arange(z_n)) % z_n
    x_order = (x + jnp.arange(x_n)) % x_n
    picked_rows = block_rows[z_order][:, x_order][:, :, core].T.reshape(-1)

    def owned_row(row, owner):
        local = row - owner * owned
        return jnp.where(jnp.logical_and(local >= 0, local < owned), local, -1).astype(jnp.int32)

    picked = pick_rows(
        tables, tables_pair, owned_row(picked_rows, a), owned_row(picked_rows, a ^ 1)
    ).reshape(x_n, z_n, rank, down_width + up_width)
    slices = picked[0]
    for e in range(1, x_n):
        slices = slices + over_x(picked[e], e)
    adapter_slices = {0: slices[0]}
    for d in range(1, z_n):
        adapter_slices[(-d) % z_n] = over_z(slices[d], d)

    def token_slice(array, j):
        return lax.dynamic_slice(array, (0, ((z + j) % z_n) * depth), (rows, depth))

    own_slices = [token_slice(tokens, j) for j in range(z_n)]
    both = [
        jnp.concatenate([own_slices[j], token_slice(tokens_pair, j)], axis=0) for j in range(z_n)
    ]
    base_turned = None
    for d in range(1, z_n):
        along_x = [from_z[d]] + [over_x(from_z[d], e) for e in range(1, x_n)]
        shard = list(along_x)
        for g in range(1, copies_n):
            shard += [over_y(v, g) for v in along_x]
        part = jnp.dot(
            both[(-d) % z_n],
            jnp.concatenate(shard, axis=1),
            preferred_element_type=jnp.float32,
        )
        base_turned = part if base_turned is None else base_turned + part
    pieces = []
    for y_to in range(copies_n):
        for x_to in range(x_n):
            at = ((y - y_to) % copies_n) * x_n + (x - x_to) % x_n
            pieces.append(
                lax.dynamic_slice(base_turned, (0, at * unit_width), (2 * rows, unit_width))
            )
    base_half = jnp.concatenate(pieces, axis=1) + jnp.dot(
        both[0], own_half, preferred_element_type=jnp.float32
    )
    base_other = over_core(base_half[rows:])
    base_mine = base_half[:rows]
    base = jnp.where(
        core == 0,
        jnp.concatenate([base_mine, base_other], axis=1),
        jnp.concatenate([base_other, base_mine], axis=1),
    )

    my_adapter = packed_block_adapter[z * group_n + a]
    my_rank = live_adapter_rank[my_adapter]
    rank_mask = (jnp.arange(rank, dtype=jnp.int32) < my_rank).astype(jnp.float32)
    adapter_scale = ADAPTER_STRENGTH / my_rank.astype(jnp.float32)
    low = None
    for j in range(z_n):
        part = lax.dot_general(
            own_slices[j],
            adapter_slices[j][:, :down_width],
            (((1,), (1,)), ((), ())),
            preferred_element_type=jnp.float32,
        )
        low = part if low is None else low + part
    low = (low * rank_mask).astype(jnp.bfloat16)
    up_stack = jnp.stack([adapter_slices[j][:, down_width:] for j in range(z_n)])
    up = jnp.concatenate(
        [
            lax.dynamic_index_in_dim(up_stack, (f - z) % z_n, 0, keepdims=False)
            for f in range(z_n)
        ],
        axis=1,
    )
    before_norm_keys = base + adapter_scale * jnp.dot(
        low, up, preferred_element_type=jnp.float32
    )
    positions = doc_positions(document_numbers)
    cosine_part, sine_part = rope_tables(positions, key_norm_gain.shape[0])

    def rotate(values):
        return keys_from(values, cosine_part, sine_part, key_norm_gain)

    rotated, pullback = jax.vjp(rotate, before_norm_keys)
    pre_norm_gradient = pullback(rotated_key_gradient.astype(jnp.float32))[0]
    scaled = (adapter_scale * pre_norm_gradient).astype(jnp.bfloat16)
    grad_low = lax.dot_general(
        scaled, up, (((1,), (1,)), ((), ())), preferred_element_type=jnp.float32
    )
    grad_low = (grad_low * rank_mask).astype(jnp.bfloat16)
    part_up = lax.dot_general(
        low, scaled, (((0,), (0,)), ((), ())), preferred_element_type=jnp.float32
    ).astype(jnp.bfloat16)
    sent = []
    for j in range(z_n):
        part_down = lax.dot_general(
            grad_low, own_slices[j], (((0,), (0,)), ((), ())), preferred_element_type=jnp.float32
        ).astype(jnp.bfloat16)
        part_up_slice = lax.dynamic_slice(
            part_up, (0, ((z + j) % z_n) * up_width), (rank, up_width)
        )
        sent.append(jnp.concatenate([part_down, part_up_slice], axis=1))
    here = jnp.stack([sent[0]] + [over_z(sent[d], d) for d in range(1, z_n)])
    along_x = [here] + [over_x(here, e) for e in range(1, x_n)]
    blocks, owners = [], []
    z_back = (z - jnp.arange(z_n)) % z_n
    for e in range(x_n):
        blocks += [along_x[e], over_core(along_x[e])]
        for other in range(2):
            owners.append(block_rows[z_back, (x - e) % x_n, core ^ other])
    grad_down, grad_up = owner_sum(
        blocks, (jnp.concatenate(owners) - a * owned).astype(jnp.int32), owned, down_width
    )
    return (rotated.astype(jnp.bfloat16), grad_down, grad_up)


def solution(mesh):
    return jax.shard_map(
        per_device,
        mesh=mesh,
        in_specs=(
            P(("copies", "fsdp", "adapter"), None),
            P("fsdp", None),
            P(),
            P("adapter", None, "fsdp"),
            P("adapter", None, "fsdp"),
            P("copies"),
            P(),
            P(),
            P(("copies", "fsdp", "adapter")),
            P(("copies", "fsdp", "adapter"), None),
        ),
        out_specs=(
            P(("copies", "fsdp", "adapter"), None),
            P(("copies", "adapter"), None, "fsdp"),
            P(("copies", "adapter"), None, "fsdp"),
        ),
        check_vma=False,
    )
```

```python
import functools

import jax
import jax.numpy as jnp
from jax import lax
from jax.experimental import pallas as pl
from jax.experimental.pallas import tpu as pltpu
from jax.sharding import PartitionSpec as P

BLOCK_LENGTH = 256
ADAPTER_STRENGTH = 16.0
ROPE_BASE = 1000000.0


def rope_tables(positions, head_size):
    half_head = head_size // 2
    steps_iota = jnp.arange(half_head, dtype=jnp.float32)
    frequency = jnp.exp(-jnp.log(jnp.float32(ROPE_BASE)) * 2.0 * steps_iota / head_size)
    angles = positions.astype(jnp.float32)[:, None] * frequency[None, :]
    return (jnp.cos(angles), jnp.sin(angles))


def doc_positions(document_numbers):
    count = document_numbers.shape[0]
    index_iota = jnp.arange(count, dtype=jnp.int32)
    previous = jnp.concatenate([document_numbers[:1], document_numbers[:-1]])
    doc_start = jnp.logical_or(index_iota % BLOCK_LENGTH == 0, document_numbers != previous)
    first_index = lax.cummax(jnp.where(doc_start, index_iota, 0), axis=0)
    return index_iota - first_index


def block_row(numbers, blocks, z_to, group_to, group_n):
    return numbers[2 + blocks + numbers[2 + z_to * group_n + group_to]]


def pick_kernel(sizes, numbers, down_ref, up_ref, *refs):
    x_n, z_n = sizes
    out_refs, (down_buffer, up_buffer, semaphores) = refs[: 2 * x_n], refs[2 * x_n :]
    owned = down_ref.shape[0]
    z, a = numbers[0], numbers[1]
    x, core = a // 2, a % 2

    def for_block(n, act):
        pair, e, j = n // (x_n * z_n), n // z_n % x_n, n % z_n
        group_to = ((x + e) % x_n) * 2 + (core + pair) % 2
        row = block_row(numbers, 2 * x_n * z_n, (z + j) % z_n, group_to, 2 * x_n) - a * owned
        hit = jnp.logical_and(row >= 0, row < owned)

        @pl.when(hit)
        def _():
            act(pltpu.make_async_copy(down_ref.at[row], down_buffer.at[n], semaphores.at[0, n]))
            act(pltpu.make_async_copy(up_ref.at[row], up_buffer.at[n], semaphores.at[1, n]))

        return hit

    def start(n, carry):
        for_block(n, lambda copy: copy.start())
        return carry

    lax.fori_loop(0, 2 * x_n * z_n, start, 0)
    for m in range(2 * x_n):

        def finish(j, carry, m=m):
            n = m * z_n + j
            hit = for_block(n, lambda copy: copy.wait())

            @pl.when(hit)
            def _():
                out_refs[m][j] = jnp.concatenate([down_buffer[n], up_buffer[n]], axis=1)

            @pl.when(jnp.logical_not(hit))
            def _():
                out_refs[m][j] = jnp.zeros_like(out_refs[m][j])

            return carry

        lax.fori_loop(0, z_n, finish, 0)


def pick_rows(sizes, numbers, down, up):
    x_n, z_n = sizes
    count = 2 * x_n * z_n
    _, rank, down_width = down.shape
    up_width = up.shape[2]
    return pl.pallas_call(
        functools.partial(pick_kernel, sizes),
        in_specs=[pl.BlockSpec(memory_space=pltpu.SMEM)]
        + [pl.BlockSpec(memory_space=pltpu.HBM)] * 2,
        out_specs=[pl.BlockSpec(memory_space=pltpu.VMEM)] * (2 * x_n),
        out_shape=[jax.ShapeDtypeStruct((z_n, rank, down_width + up_width), down.dtype)]
        * (2 * x_n),
        scratch_shapes=[
            pltpu.VMEM((count, rank, down_width), down.dtype),
            pltpu.VMEM((count, rank, up_width), down.dtype),
            pltpu.SemaphoreType.DMA((2, count)),
        ],
        compiler_params=pltpu.CompilerParams(vmem_limit_bytes=24 * 1024 * 1024),
    )(numbers, down, up)


def owner_sum_kernel(sizes, groups, numbers, *refs):
    x_n, z_n = sizes
    count = x_n * 2 * len(groups)
    block_refs, down_ref, up_ref = refs[:count], refs[count], refs[count + 1]
    owned, _, down_width = down_ref.shape
    z, a = numbers[0], numbers[1]
    x, core = a // 2, a % 2
    down_ref[...] = jnp.zeros_like(down_ref)
    up_ref[...] = jnp.zeros_like(up_ref)
    i = 0
    for group in groups:
        for e in range(x_n):
            for pair in range(2):
                group_from = ((x - e + x_n) % x_n) * 2 + (core + pair) % 2

                def one(k, carry, i=i, first=group[0], group_from=group_from):
                    z_from = (z - first - k + z_n) % z_n
                    row = block_row(numbers, 2 * x_n * z_n, z_from, group_from, 2 * x_n)
                    row = row - a * owned

                    @pl.when(jnp.logical_and(row >= 0, row < owned))
                    def _():
                        block = block_refs[i][k].astype(jnp.float32)
                        down_ref[row] += block[:, :down_width]
                        up_ref[row] += block[:, down_width:]

                    return carry

                if len(group) == 1:
                    one(0, 0)
                else:
                    lax.fori_loop(0, len(group), one, 0)
                i += 1


def owner_sum(sizes, groups, numbers, blocks, owned, down_width):
    _, rank, width = blocks[0].shape
    tile = 16
    smem = pl.BlockSpec(memory_space=pltpu.SMEM)
    return pl.pallas_call(
        functools.partial(owner_sum_kernel, sizes, groups),
        grid=(rank // tile,),
        in_specs=[smem]
        + [pl.BlockSpec((b.shape[0], tile, width), lambda t: (0, t, 0)) for b in blocks],
        out_specs=[
            pl.BlockSpec((owned, tile, down_width), lambda t: (0, t, 0)),
            pl.BlockSpec((owned, tile, width - down_width), lambda t: (0, t, 0)),
        ],
        out_shape=[
            jax.ShapeDtypeStruct((owned, rank, down_width), jnp.float32),
            jax.ShapeDtypeStruct((owned, rank, width - down_width), jnp.float32),
        ],
        compiler_params=pltpu.CompilerParams(vmem_limit_bytes=12 * 1024 * 1024),
    )(numbers, *blocks)


def low_kernel(
    z_n, place_ref, rank_ref, tokens_ref, *refs,
):
    slice_refs = refs[:z_n]
    low_ref, up_ref, update_ref, tokens_buffer, semaphore = refs[z_n:]
    fetch = pltpu.make_async_copy(tokens_ref, tokens_buffer, semaphore)
    fetch.start()
    z = place_ref[0]
    rank, depth = low_ref.shape[1], tokens_ref.shape[1] // z_n
    up_width = up_ref.shape[1] // z_n
    for j in range(z_n):
        f = (z + j) % z_n
        up_ref[:, pl.ds(pl.multiple_of(f * up_width, 128), up_width)] = slice_refs[j][:, depth:]
    fetch.wait()
    low = None
    for j in range(z_n):
        f = (z + j) % z_n
        part = lax.dot_general(
            tokens_buffer[:, pl.ds(pl.multiple_of(f * depth, 128), depth)],
            slice_refs[j][:, :depth],
            (((1,), (1,)), ((), ())),
            preferred_element_type=jnp.float32,
        )
        low = part if low is None else low + part
    live = lax.broadcasted_iota(jnp.int32, (1, rank), 1) < rank_ref[...]
    low = jnp.where(live, low, 0.0).astype(jnp.bfloat16)
    low_ref[...] = low
    scale = ADAPTER_STRENGTH / rank_ref[...].astype(jnp.float32)
    update_ref[...] = scale * jnp.dot(
        low, up_ref[...], preferred_element_type=jnp.float32
    )


def low_and_update(z_n, place, live_rank, tokens, slices):
    rows, width = tokens.shape
    rank, slice_width = slices[0].shape
    depth = width // z_n
    up_width = slice_width - depth
    features = up_width * z_n
    smem = pl.BlockSpec(memory_space=pltpu.SMEM)
    vmem = pl.BlockSpec(memory_space=pltpu.VMEM)
    if depth % 128 == 0 and up_width % 128 == 0:
        return pl.pallas_call(
            functools.partial(low_kernel, z_n),
            in_specs=[smem, vmem, pl.BlockSpec(memory_space=pltpu.HBM)] + [vmem] * z_n,
            out_specs=[vmem] * 3,
            out_shape=[
                jax.ShapeDtypeStruct((rows, rank), jnp.bfloat16),
                jax.ShapeDtypeStruct((rank, features), jnp.bfloat16),
                jax.ShapeDtypeStruct((rows, features), jnp.float32),
            ],
            scratch_shapes=[pltpu.VMEM((rows, width), tokens.dtype), pltpu.SemaphoreType.DMA],
            compiler_params=pltpu.CompilerParams(vmem_limit_bytes=16 * 1024 * 1024),
        )(place, live_rank, tokens, *slices)
    z = place[0]
    stack = jnp.stack(slices)[(jnp.arange(z_n) - z) % z_n]
    down = jnp.swapaxes(stack[:, :, :depth], 0, 1).reshape(rank, width)
    up = jnp.swapaxes(stack[:, :, depth:], 0, 1).reshape(rank, features)
    low = lax.dot_general(
        tokens, down, (((1,), (1,)), ((), ())), preferred_element_type=jnp.float32
    )
    live = jnp.arange(rank, dtype=jnp.int32)[None, :] < live_rank
    low = jnp.where(live, low, 0.0).astype(jnp.bfloat16)
    scale = ADAPTER_STRENGTH / live_rank.astype(jnp.float32)
    return low, up, scale * jnp.dot(low, up, preferred_element_type=jnp.float32)


def norm_kernel(
    z_n, units, place_ref, columns_ref, rank_ref, *refs,
):
    base_refs, refs = refs[: 2 * units], refs[2 * units :]
    update_ref, low_ref, up_ref, cosine_ref, sine_ref, gain_ref = refs[:6]
    gradient_ref, tokens_ref, keys_ref = refs[6:9]
    refs = refs[9:]
    sent_refs, (tokens_buffer, gradient_buffer, part_up, semaphores) = refs[:-4], refs[-4:]
    fetch_gradient = pltpu.make_async_copy(gradient_ref, gradient_buffer, semaphores.at[0])
    fetch_tokens = pltpu.make_async_copy(tokens_ref, tokens_buffer, semaphores.at[1])
    fetch_gradient.start()
    fetch_tokens.start()
    z, core = place_ref[0], place_ref[1] % 2
    scale = ADAPTER_STRENGTH / rank_ref[...].astype(jnp.float32)
    head = gain_ref.shape[1]
    width = base_refs[0].shape[1]
    half = units * width
    low = low_ref[...]
    cosine, sine, gain = cosine_ref[...], sine_ref[...], gain_ref[...]
    gain_cosine, gain_sine = cosine * gain, sine * pltpu.roll(gain, head // 2, 1)
    grad_low = None
    fetch_gradient.wait()
    for n, base_ref in enumerate(base_refs):
        first = (core if n < units else 1 - core) * half + columns_ref[n % units]
        for i in range(width // head):
            at = pl.ds(pl.multiple_of(first + i * head, 128), head)
            up = up_ref[:, at]
            pre = base_ref[:, i * head : (i + 1) * head] + update_ref[:, at]
            inverse = lax.rsqrt(jnp.mean(pre * pre, axis=1, keepdims=True) + 1e-06)
            unit = pre * inverse
            keys = unit * gain_cosine + pltpu.roll(unit, head // 2, 1) * gain_sine
            keys_ref[:, at] = keys.astype(keys_ref.dtype)
            gradient = gradient_buffer[:, at].astype(jnp.float32)
            turned = gain * (gradient * cosine - pltpu.roll(gradient, head // 2, 1) * sine)
            along = jnp.mean(turned * unit, axis=1, keepdims=True)
            scaled = ((scale * inverse) * (turned - unit * along)).astype(jnp.bfloat16)
            part_low = lax.dot_general(
                scaled, up, (((1,), (1,)), ((), ())), preferred_element_type=jnp.float32
            )
            grad_low = part_low if grad_low is None else grad_low + part_low
            part_up[:, at] = lax.dot_general(
                low, scaled, (((0,), (0,)), ((), ())), preferred_element_type=jnp.float32
            ).astype(part_up.dtype)
    live = lax.broadcasted_iota(jnp.int32, (1, low.shape[1]), 1) < rank_ref[...]
    grad_low = jnp.where(live, grad_low, 0.0).astype(jnp.bfloat16)
    fetch_tokens.wait()
    if len(sent_refs) == 2:
        sent_refs[0][...] = lax.dot_general(
            grad_low, tokens_buffer[...], (((0,), (0,)), ((), ())),
            preferred_element_type=jnp.float32,
        ).astype(jnp.bfloat16)
        sent_refs[1][...] = part_up[...]
        return
    depth = tokens_ref.shape[1] // z_n
    up_width = part_up.shape[1] // z_n
    for j in range(z_n):
        f = (z + j) % z_n
        sent_refs[j][:, :depth] = lax.dot_general(
            grad_low,
            tokens_buffer[:, pl.ds(pl.multiple_of(f * depth, 128), depth)],
            (((0,), (0,)), ((), ())),
            preferred_element_type=jnp.float32,
        ).astype(jnp.bfloat16)
        sent_refs[j][:, depth:] = part_up[:, pl.ds(pl.multiple_of(f * up_width, 128), up_width)]


def norm_and_back(
    z_n, place, columns, live_rank, bases, update, low, up, cosine, sine, gain,
    gradient, tokens,
):
    rows, features = gradient.shape
    rank = up.shape[0]
    width = tokens.shape[1]
    depth, up_width = width // z_n, features // z_n
    aligned = depth % 128 == 0 and up_width % 128 == 0
    if aligned:
        sent = [jax.ShapeDtypeStruct((rank, depth + up_width), jnp.bfloat16)] * z_n
    else:
        sent = [
            jax.ShapeDtypeStruct((rank, width), jnp.bfloat16),
            jax.ShapeDtypeStruct((rank, features), jnp.bfloat16),
        ]
    smem = pl.BlockSpec(memory_space=pltpu.SMEM)
    vmem = pl.BlockSpec(memory_space=pltpu.VMEM)
    hbm = pl.BlockSpec(memory_space=pltpu.HBM)
    outs = pl.pallas_call(
        functools.partial(norm_kernel, z_n, len(bases) // 2),
        in_specs=[smem] * 2 + [vmem] * (len(bases) + 7) + [hbm] * 2,
        out_specs=[vmem] * (1 + len(sent)),
        out_shape=[jax.ShapeDtypeStruct((rows, features), jnp.bfloat16)] + sent,
        scratch_shapes=[
            pltpu.VMEM((rows, width), tokens.dtype),
            pltpu.VMEM((rows, features), gradient.dtype),
            pltpu.VMEM((rank, features), jnp.bfloat16),
            pltpu.SemaphoreType.DMA((2,)),
        ],
        compiler_params=pltpu.CompilerParams(vmem_limit_bytes=24 * 1024 * 1024),
    )(
        place, columns, live_rank, *bases, update, low, up, cosine, sine, gain,
        gradient, tokens,
    )
    if aligned:
        return outs[0], outs[1:]
    z = place[0]
    return outs[0], [
        jnp.concatenate(
            [
                lax.dynamic_slice(outs[1], (0, ((z + j) % z_n) * depth), (rank, depth)),
                lax.dynamic_slice(outs[2], (0, ((z + j) % z_n) * up_width), (rank, up_width)),
            ],
            axis=1,
        )
        for j in range(z_n)
    ]


def dots_kernel(z_n, shards, totals, place_ref, tokens_ref, pair_ref, *refs):
    count = sum(len(group) for group in shards)
    unit_refs, refs = refs[:count], refs[count:]
    total_refs, out_refs = refs[: 2 * totals], refs[2 * totals : 2 * totals + 2 * len(shards)]
    buffers, semaphores = refs[-4:-2], refs[-2:]
    depth = unit_refs[0].shape[0]
    only = {d for group in shards for d in group}
    fetches = []
    for side, ref in enumerate((tokens_ref, pair_ref)):
        if len(only) == 1:
            at = pl.multiple_of(((place_ref[0] - min(only) + z_n) % z_n) * depth, 128)
            ref = ref.at[:, pl.ds(at, depth)]
        fetches.append(pltpu.make_async_copy(ref, buffers[side], semaphores[side]))
        fetches[side].start()
    for side in range(2):
        fetches[side].wait()
        n = 0
        for u, group in enumerate(shards):
            value = None
            for d in group:
                at = pl.multiple_of(((place_ref[0] - d + z_n) % z_n) * depth, 128)
                left = (
                    buffers[side][...]
                    if len(only) == 1
                    else buffers[side][:, pl.ds(at, depth)]
                )
                part = jnp.dot(left, unit_refs[n][...], preferred_element_type=jnp.float32)
                value = part if value is None else value + part
                n += 1
            if totals:
                value = value + total_refs[side * totals + u][...]
            out_refs[side * len(shards) + u][...] = value


def add_dots(z_n, place, tokens, pair, shards, units, totals):
    rows = tokens.shape[0]
    depth, width = units[0][0].shape
    count = len(shards)
    if depth % 128 or width % 128:
        outs = []
        for side, array in enumerate((tokens, pair)):
            for u, group in enumerate(shards):
                value = totals[side * count + u] if totals else 0.0
                for d, unit in zip(group, units[u]):
                    at = ((place[0] - d) % z_n) * depth
                    value = value + jnp.dot(
                        lax.dynamic_slice(array, (0, at), (rows, depth)),
                        unit,
                        preferred_element_type=jnp.float32,
                    )
                outs.append(value)
        return outs
    hbm = pl.BlockSpec(memory_space=pltpu.HBM)
    vmem = pl.BlockSpec(memory_space=pltpu.VMEM)
    flat = [unit for group in units for unit in group]
    only = {d for group in shards for d in group}
    buffer = pltpu.VMEM((rows, depth if len(only) == 1 else tokens.shape[1]), tokens.dtype)
    outs = pl.pallas_call(
        functools.partial(dots_kernel, z_n, shards, len(totals) // 2),
        in_specs=[pl.BlockSpec(memory_space=pltpu.SMEM), hbm, hbm]
        + [vmem] * (len(flat) + len(totals)),
        out_specs=[vmem] * (2 * count),
        out_shape=[jax.ShapeDtypeStruct((rows, width), jnp.float32)] * (2 * count),
        scratch_shapes=[buffer, buffer, pltpu.SemaphoreType.DMA, pltpu.SemaphoreType.DMA],
        compiler_params=pltpu.CompilerParams(vmem_limit_bytes=20 * 1024 * 1024),
    )(place, tokens, pair, *flat, *totals)
    return list(outs)


def after(value, *others):
    return lax.optimization_barrier((value,) + others)[0]


def per_device(
    tokens,
    frozen_key_weight,
    key_norm_gain,
    adapter_down_weight,
    adapter_up_weight,
    packed_block_adapter,
    adapter_storage_row,
    live_adapter_rank,
    document_numbers,
    rotated_key_gradient,
):
    rows = tokens.shape[0]
    features = rotated_key_gradient.shape[1]
    depth = frozen_key_weight.shape[0]
    owned, rank, down_width = adapter_down_weight.shape
    up_width = adapter_up_weight.shape[2]
    copies_n = lax.axis_size("copies")
    z_n = lax.axis_size("fsdp")
    group_n = lax.axis_size("adapter")
    x_n = group_n // 2
    y = lax.axis_index("copies")
    z = lax.axis_index("fsdp")
    a = lax.axis_index("adapter")
    x, core = a // 2, a % 2

    def over_core(v):
        return lax.ppermute(v, "adapter", [(i, i ^ 1) for i in range(group_n)])

    def over_x(v, e):
        return lax.ppermute(
            v, "adapter", [(i, ((i // 2 + e) % x_n) * 2 + i % 2) for i in range(group_n)]
        )

    def over_y(v, g):
        return lax.ppermute(v, "copies", [(i, (i + g) % copies_n) for i in range(copies_n)])

    def over_z(v, d):
        return lax.ppermute(v, "fsdp", [(i, (i + d) % z_n) for i in range(z_n)])

    half = features // 2
    units = copies_n * x_n
    unit_width = half // units

    def unit_at(y_at, x_at):
        at = core * half + (y_at * x_n + x_at) * unit_width
        return lax.dynamic_slice(frozen_key_weight, (0, at), (depth, unit_width))

    unit = unit_at(y, x)
    sizes = (x_n, z_n)
    place = jnp.stack([z, a]).astype(jnp.int32)
    numbers = jnp.concatenate([place, packed_block_adapter, adapter_storage_row])
    shifts = sorted(range(1, z_n), key=lambda d: min(d, z_n - d))
    final = len(shifts) - 1

    tokens_pair = over_core(tokens)
    picked = pick_rows(sizes, numbers, adapter_down_weight, adapter_up_weight)
    taken = [over_core(picked[x_n + e]) for e in range(x_n)]
    away = [picked[e] + after(taken[e], tokens_pair, taken[0]) for e in range(1, x_n)]
    slices = picked[0] + taken[0]
    from_z = {d: over_z(unit if k < 2 else after(unit, *away), d) for k, d in enumerate(shifts)}
    for e in range(1, x_n):
        slices = slices + over_x(away[e - 1], e)

    documents, packed, ranks, gain = lax.optimization_barrier(
        (
            document_numbers,
            packed_block_adapter,
            live_adapter_rank,
            key_norm_gain,
            away[0],
        )
    )[:4]
    mine = jnp.arange(packed.shape[0], dtype=jnp.int32) == z * group_n + a
    mine = jnp.arange(ranks.shape[0], dtype=jnp.int32) == jnp.sum(jnp.where(mine, packed, 0))
    live_rank = jnp.sum(jnp.where(mine, ranks, 0)).reshape(1, 1)
    cosine_part, sine_part = rope_tables(doc_positions(documents), key_norm_gain.shape[0])
    cosine = jnp.concatenate([cosine_part, cosine_part], axis=1)
    sine = jnp.concatenate([-sine_part, sine_part], axis=1)

    frozen_key_weight = after(frozen_key_weight, away[0])
    own_units = [
        unit_at((y - g) % copies_n, (x - e) % x_n) for g in range(copies_n) for e in range(x_n)
    ]
    along_x, along_y, diagonal = [], [], []
    for k, d in enumerate(shifts):
        gate = away[0] if k < 2 else along_y[k - 2][-1]
        along_y.append([over_y(after(from_z[d], gate), g) for g in range(1, copies_n)])
    for k, d in enumerate(shifts):
        gate = (away[0], along_y[0][-1], slices)[min(k, 2)]
        along_x.append([over_x(after(from_z[d], gate), e) for e in range(1, x_n)])
    for k, d in enumerate(shifts):
        if k < final:
            gate = along_y[k + 1][-1]
            diagonal.append(
                [[over_y(after(v, gate), g) for v in along_x[k]] for g in range(1, copies_n)]
            )
    adapter_slices = {0: slices[0]}
    for k, d in enumerate(shifts):
        gates = (along_x[0][-1],) if k >= 2 else ()
        adapter_slices[(-d) % z_n] = over_z(after(slices[d], *gates), d)
    diagonal.append(
        [
            [over_x(after(v, along_x[max(final - 1, 0)][-1]), e) for e in range(1, x_n)]
            for v in along_y[final]
        ]
    )
    shards = {0: own_units}
    for k, d in enumerate(shifts):
        shards[d] = [from_z[d]] + along_x[k]
        for g in range(1, copies_n):
            shards[d] += [along_y[k][g - 1]] + diagonal[k][g - 1]
    order = [0] + shifts
    groups = [order] * (units - 1) + [order[:-1]]
    first = add_dots(
        z_n,
        after(place, cosine, sine, live_rank, *adapter_slices.values()),
        tokens,
        tokens_pair,
        groups,
        [[shards[d][u] for d in group] for u, group in enumerate(groups)],
        [],
    )
    last = add_dots(
        z_n,
        place,
        tokens,
        tokens_pair,
        [order[-1:]],
        [[shards[order[-1]][-1]]],
        [first[units - 1], first[-1]],
    )
    bases = first[: units - 1] + [last[0]]
    bases += [over_core(v) for v in first[units:-1] + [last[1]]]
    head = key_norm_gain.shape[0]
    columns = [
        (((y - g) % copies_n) * x_n + (x - e) % x_n) * unit_width
        for g in range(copies_n)
        for e in range(x_n)
    ]
    if unit_width % head:
        natural = []
        for side in (bases[:units], bases[units:]):
            stack = jnp.stack(side)
            order = jnp.stack(
                [
                    ((y - y_at) % copies_n) * x_n + (x - x_at) % x_n
                    for y_at in range(copies_n)
                    for x_at in range(x_n)
                ]
            )
            whole = jnp.swapaxes(stack[order], 0, 1).reshape(rows, half)
            natural.append(whole)
        bases = natural
        columns = [jnp.zeros_like(z)]

    low, up, update = low_and_update(
        z_n,
        place,
        live_rank,
        tokens,
        [adapter_slices[j] for j in range(z_n)],
    )
    rotated, sent = norm_and_back(
        z_n,
        place,
        jnp.stack(columns).astype(jnp.int32),
        live_rank,
        bases,
        update,
        low,
        up,
        cosine,
        sine,
        gain[None],
        rotated_key_gradient,
        tokens,
    )
    order = [0] + shifts if z_n <= 4 else list(range(z_n))
    step = -(-z_n // 4)
    groups = [tuple(order[k : k + step]) for k in range(0, z_n, step)]
    arrived = {d: sent[0] if d == 0 else over_z(sent[d], d) for d in order}
    blocks = []
    for group in groups:
        if len(group) == 1:
            here = arrived[group[0]][None]
        else:
            here = jnp.stack([arrived[d] for d in group])
        for e in range(x_n):
            there = over_x(here, e) if e else here
            blocks += [there, over_core(there)]
    grad_down, grad_up = owner_sum(
        sizes,
        groups,
        numbers,
        blocks,
        owned,
        down_width,
    )
    return (rotated, grad_down, grad_up)


def solution(mesh):
    return jax.shard_map(
        per_device,
        mesh=mesh,
        in_specs=(
            P(("copies", "fsdp", "adapter"), None),
            P("fsdp", None),
            P(),
            P("adapter", None, "fsdp"),
            P("adapter", None, "fsdp"),
            P("copies"),
            P(),
            P(),
            P(("copies", "fsdp", "adapter")),
            P(("copies", "fsdp", "adapter"), None),
        ),
        out_specs=(
            P(("copies", "fsdp", "adapter"), None),
            P(("copies", "adapter"), None, "fsdp"),
            P(("copies", "adapter"), None, "fsdp"),
        ),
        check_vma=False,
    )
```

```python
import functools

import jax
import jax.numpy as jnp
from jax import lax
from jax.experimental import pallas as pl
from jax.experimental.pallas import tpu as pltpu
from jax.sharding import PartitionSpec as P

BLOCK_LENGTH = 256
ADAPTER_STRENGTH = 16.0
ROPE_BASE = 1000000.0


def rope_tables(positions, head_size):
    half_head = head_size // 2
    steps_iota = jnp.arange(half_head, dtype=jnp.float32)
    frequency = jnp.exp(-jnp.log(jnp.float32(ROPE_BASE)) * 2.0 * steps_iota / head_size)
    angles = positions.astype(jnp.float32)[:, None] * frequency[None, :]
    return (jnp.cos(angles), jnp.sin(angles))


def doc_positions(document_numbers):
    count = document_numbers.shape[0]
    index_iota = jnp.arange(count, dtype=jnp.int32)
    previous = jnp.concatenate([document_numbers[:1], document_numbers[:-1]])
    doc_start = jnp.logical_or(index_iota % BLOCK_LENGTH == 0, document_numbers != previous)
    first_index = lax.cummax(jnp.where(doc_start, index_iota, 0), axis=0)
    return index_iota - first_index


def block_row(numbers, blocks, z_to, group_to, group_n):
    return numbers[2 + blocks + numbers[2 + z_to * group_n + group_to]]


def pick_kernel(sizes, numbers, down_ref, up_ref, *refs):
    x_n, z_n = sizes
    out_refs, (down_buffer, up_buffer, semaphores) = refs[: 2 * x_n], refs[2 * x_n :]
    owned = down_ref.shape[0]
    z, a = numbers[0], numbers[1]
    x, core = a // 2, a % 2

    def for_block(n, act):
        pair, e, j = n // (x_n * z_n), n // z_n % x_n, n % z_n
        group_to = ((x + e) % x_n) * 2 + (core + pair) % 2
        row = block_row(numbers, 2 * x_n * z_n, (z + j) % z_n, group_to, 2 * x_n) - a * owned
        hit = jnp.logical_and(row >= 0, row < owned)

        @pl.when(hit)
        def _():
            act(pltpu.make_async_copy(down_ref.at[row], down_buffer.at[n], semaphores.at[0, n]))
            act(pltpu.make_async_copy(up_ref.at[row], up_buffer.at[n], semaphores.at[1, n]))

        return hit

    def start(n, carry):
        for_block(n, lambda copy: copy.start())
        return carry

    lax.fori_loop(0, 2 * x_n * z_n, start, 0)
    for m in range(2 * x_n):

        def finish(j, carry, m=m):
            n = m * z_n + j
            hit = for_block(n, lambda copy: copy.wait())

            @pl.when(hit)
            def _():
                out_refs[m][j] = jnp.concatenate([down_buffer[n], up_buffer[n]], axis=1)

            @pl.when(jnp.logical_not(hit))
            def _():
                out_refs[m][j] = jnp.zeros_like(out_refs[m][j])

            return carry

        lax.fori_loop(0, z_n, finish, 0)


def pick_rows(sizes, numbers, down, up):
    x_n, z_n = sizes
    count = 2 * x_n * z_n
    _, rank, down_width = down.shape
    up_width = up.shape[2]
    return pl.pallas_call(
        functools.partial(pick_kernel, sizes),
        in_specs=[pl.BlockSpec(memory_space=pltpu.SMEM)]
        + [pl.BlockSpec(memory_space=pltpu.HBM)] * 2,
        out_specs=[pl.BlockSpec(memory_space=pltpu.VMEM)] * (2 * x_n),
        out_shape=[jax.ShapeDtypeStruct((z_n, rank, down_width + up_width), down.dtype)]
        * (2 * x_n),
        scratch_shapes=[
            pltpu.VMEM((count, rank, down_width), down.dtype),
            pltpu.VMEM((count, rank, up_width), down.dtype),
            pltpu.SemaphoreType.DMA((2, count)),
        ],
        compiler_params=pltpu.CompilerParams(vmem_limit_bytes=56 * 1024 * 1024),
    )(numbers, down, up)


def owner_sum_kernel(sizes, groups, numbers, *refs):
    x_n, z_n = sizes
    count = x_n * 2 * len(groups)
    block_refs, down_ref, up_ref = refs[:count], refs[count], refs[count + 1]
    owned, tile, down_width = down_ref.shape
    first_row = pl.multiple_of(pl.program_id(0) * tile, tile)
    z, a = numbers[0], numbers[1]
    x, core = a // 2, a % 2
    down_ref[...] = jnp.zeros_like(down_ref)
    up_ref[...] = jnp.zeros_like(up_ref)
    i = 0
    for group in groups:
        for e in range(x_n):
            for pair in range(2):
                group_from = ((x - e + x_n) % x_n) * 2 + (core + pair) % 2

                def one(k, carry, i=i, first=group[0], group_from=group_from):
                    z_from = (z - first - k + z_n) % z_n
                    row = block_row(numbers, 2 * x_n * z_n, z_from, group_from, 2 * x_n)
                    row = row - a * owned

                    @pl.when(jnp.logical_and(row >= 0, row < owned))
                    def _():
                        block = block_refs[i][k, pl.ds(first_row, tile), :].astype(jnp.float32)
                        down_ref[row] += block[:, :down_width]
                        up_ref[row] += block[:, down_width:]

                    return carry

                if len(group) == 1:
                    one(0, 0)
                else:
                    lax.fori_loop(0, len(group), one, 0)
                i += 1


def owner_sum(sizes, groups, numbers, blocks, owned, down_width):
    _, rank, width = blocks[0].shape
    tile = 16
    smem = pl.BlockSpec(memory_space=pltpu.SMEM)
    return pl.pallas_call(
        functools.partial(owner_sum_kernel, sizes, groups),
        grid=(rank // tile,),
        in_specs=[smem]
        + [pl.BlockSpec(memory_space=pltpu.VMEM)] * len(blocks),
        out_specs=[
            pl.BlockSpec((owned, tile, down_width), lambda t: (0, t, 0)),
            pl.BlockSpec((owned, tile, width - down_width), lambda t: (0, t, 0)),
        ],
        out_shape=[
            jax.ShapeDtypeStruct((owned, rank, down_width), jnp.float32),
            jax.ShapeDtypeStruct((owned, rank, width - down_width), jnp.float32),
        ],
        compiler_params=pltpu.CompilerParams(vmem_limit_bytes=12 * 1024 * 1024),
    )(numbers, *blocks)


def low_kernel(
    z_n, place_ref, rank_ref, tokens_ref, *refs,
):
    slice_refs = refs[:z_n]
    low_ref, up_ref, update_ref, tokens_buffer, semaphore = refs[z_n:]
    fetch = pltpu.make_async_copy(tokens_ref, tokens_buffer, semaphore)
    fetch.start()
    z = place_ref[0]
    rank, depth = low_ref.shape[1], tokens_ref.shape[1] // z_n
    up_width = up_ref.shape[1] // z_n
    for j in range(z_n):
        f = (z + j) % z_n
        up_ref[:, pl.ds(pl.multiple_of(f * up_width, 128), up_width)] = slice_refs[j][:, depth:]
    fetch.wait()
    low = None
    for j in range(z_n):
        f = (z + j) % z_n
        part = lax.dot_general(
            tokens_buffer[:, pl.ds(pl.multiple_of(f * depth, 128), depth)],
            slice_refs[j][:, :depth],
            (((1,), (1,)), ((), ())),
            preferred_element_type=jnp.float32,
        )
        low = part if low is None else low + part
    live = lax.broadcasted_iota(jnp.int32, (1, rank), 1) < rank_ref[...]
    low = jnp.where(live, low, 0.0).astype(jnp.bfloat16)
    low_ref[...] = low
    scale = ADAPTER_STRENGTH / rank_ref[...].astype(jnp.float32)
    update_ref[...] = scale * jnp.dot(
        low, up_ref[...], preferred_element_type=jnp.float32
    )


def low_and_update(z_n, place, live_rank, tokens, slices):
    rows, width = tokens.shape
    rank, slice_width = slices[0].shape
    depth = width // z_n
    up_width = slice_width - depth
    features = up_width * z_n
    smem = pl.BlockSpec(memory_space=pltpu.SMEM)
    vmem = pl.BlockSpec(memory_space=pltpu.VMEM)
    if depth % 128 == 0 and up_width % 128 == 0:
        return pl.pallas_call(
            functools.partial(low_kernel, z_n),
            in_specs=[smem, vmem, pl.BlockSpec(memory_space=pltpu.HBM)] + [vmem] * z_n,
            out_specs=[vmem] * 3,
            out_shape=[
                jax.ShapeDtypeStruct((rows, rank), jnp.bfloat16),
                jax.ShapeDtypeStruct((rank, features), jnp.bfloat16),
                jax.ShapeDtypeStruct((rows, features), jnp.float32),
            ],
            scratch_shapes=[pltpu.VMEM((rows, width), tokens.dtype), pltpu.SemaphoreType.DMA],
            compiler_params=pltpu.CompilerParams(vmem_limit_bytes=16 * 1024 * 1024),
        )(place, live_rank, tokens, *slices)
    z = place[0]
    stack = jnp.stack(slices)[(jnp.arange(z_n) - z) % z_n]
    down = jnp.swapaxes(stack[:, :, :depth], 0, 1).reshape(rank, width)
    up = jnp.swapaxes(stack[:, :, depth:], 0, 1).reshape(rank, features)
    low = lax.dot_general(
        tokens, down, (((1,), (1,)), ((), ())), preferred_element_type=jnp.float32
    )
    live = jnp.arange(rank, dtype=jnp.int32)[None, :] < live_rank
    low = jnp.where(live, low, 0.0).astype(jnp.bfloat16)
    scale = ADAPTER_STRENGTH / live_rank.astype(jnp.float32)
    return low, up, scale * jnp.dot(low, up, preferred_element_type=jnp.float32)


def norm_kernel(
    z_n, units, place_ref, columns_ref, rank_ref, *refs,
):
    base_refs, refs = refs[: 2 * units], refs[2 * units :]
    update_ref, low_ref, up_ref, cosine_ref, sine_ref, gain_ref = refs[:6]
    gradient_ref, tokens_ref, keys_ref = refs[6:9]
    refs = refs[9:]
    sent_refs, (tokens_buffer, gradient_buffer, part_up, semaphores) = refs[:-4], refs[-4:]
    fetch_gradient = pltpu.make_async_copy(gradient_ref, gradient_buffer, semaphores.at[0])
    fetch_tokens = pltpu.make_async_copy(tokens_ref, tokens_buffer, semaphores.at[1])
    fetch_gradient.start()
    fetch_tokens.start()
    z, core = place_ref[0], place_ref[1] % 2
    scale = ADAPTER_STRENGTH / rank_ref[...].astype(jnp.float32)
    head = gain_ref.shape[1]
    width = base_refs[0].shape[1]
    half = units * width
    low = low_ref[...]
    cosine, sine, gain = cosine_ref[...], sine_ref[...], gain_ref[...]
    gain_cosine, gain_sine = cosine * gain, sine * pltpu.roll(gain, head // 2, 1)
    grad_low = None
    fetch_gradient.wait()
    for n, base_ref in enumerate(base_refs):
        first = (core if n < units else 1 - core) * half + columns_ref[n % units]
        for i in range(width // head):
            at = pl.ds(pl.multiple_of(first + i * head, 128), head)
            up = up_ref[:, at]
            pre = base_ref[:, i * head : (i + 1) * head] + update_ref[:, at]
            inverse = lax.rsqrt(jnp.mean(pre * pre, axis=1, keepdims=True) + 1e-06)
            unit = pre * inverse
            keys = unit * gain_cosine + pltpu.roll(unit, head // 2, 1) * gain_sine
            keys_ref[:, at] = keys.astype(keys_ref.dtype)
            gradient = gradient_buffer[:, at].astype(jnp.float32)
            turned = gain * (gradient * cosine - pltpu.roll(gradient, head // 2, 1) * sine)
            along = jnp.mean(turned * unit, axis=1, keepdims=True)
            scaled = ((scale * inverse) * (turned - unit * along)).astype(jnp.bfloat16)
            part_low = lax.dot_general(
                scaled, up, (((1,), (1,)), ((), ())), preferred_element_type=jnp.float32
            )
            grad_low = part_low if grad_low is None else grad_low + part_low
            part_up[:, at] = lax.dot_general(
                low, scaled, (((0,), (0,)), ((), ())), preferred_element_type=jnp.float32
            ).astype(part_up.dtype)
    live = lax.broadcasted_iota(jnp.int32, (1, low.shape[1]), 1) < rank_ref[...]
    grad_low = jnp.where(live, grad_low, 0.0).astype(jnp.bfloat16)
    fetch_tokens.wait()
    if len(sent_refs) == 2:
        sent_refs[0][...] = lax.dot_general(
            grad_low, tokens_buffer[...], (((0,), (0,)), ((), ())),
            preferred_element_type=jnp.float32,
        ).astype(jnp.bfloat16)
        sent_refs[1][...] = part_up[...]
        return
    depth = tokens_ref.shape[1] // z_n
    up_width = part_up.shape[1] // z_n
    for j in range(z_n):
        f = (z + j) % z_n
        sent_refs[j][:, :depth] = lax.dot_general(
            grad_low,
            tokens_buffer[:, pl.ds(pl.multiple_of(f * depth, 128), depth)],
            (((0,), (0,)), ((), ())),
            preferred_element_type=jnp.float32,
        ).astype(jnp.bfloat16)
        sent_refs[j][:, depth:] = part_up[:, pl.ds(pl.multiple_of(f * up_width, 128), up_width)]


def norm_and_back(
    z_n, place, columns, live_rank, bases, update, low, up, cosine, sine, gain,
    gradient, tokens,
):
    rows, features = gradient.shape
    rank = up.shape[0]
    width = tokens.shape[1]
    depth, up_width = width // z_n, features // z_n
    aligned = depth % 128 == 0 and up_width % 128 == 0
    if aligned:
        sent = [jax.ShapeDtypeStruct((rank, depth + up_width), jnp.bfloat16)] * z_n
    else:
        sent = [
            jax.ShapeDtypeStruct((rank, width), jnp.bfloat16),
            jax.ShapeDtypeStruct((rank, features), jnp.bfloat16),
        ]
    smem = pl.BlockSpec(memory_space=pltpu.SMEM)
    vmem = pl.BlockSpec(memory_space=pltpu.VMEM)
    hbm = pl.BlockSpec(memory_space=pltpu.HBM)
    outs = pl.pallas_call(
        functools.partial(norm_kernel, z_n, len(bases) // 2),
        in_specs=[smem] * 2 + [vmem] * (len(bases) + 7) + [hbm] * 2,
        out_specs=[vmem] * (1 + len(sent)),
        out_shape=[jax.ShapeDtypeStruct((rows, features), jnp.bfloat16)] + sent,
        scratch_shapes=[
            pltpu.VMEM((rows, width), tokens.dtype),
            pltpu.VMEM((rows, features), gradient.dtype),
            pltpu.VMEM((rank, features), jnp.bfloat16),
            pltpu.SemaphoreType.DMA((2,)),
        ],
        compiler_params=pltpu.CompilerParams(vmem_limit_bytes=24 * 1024 * 1024),
    )(
        place, columns, live_rank, *bases, update, low, up, cosine, sine, gain,
        gradient, tokens,
    )
    if aligned:
        return outs[0], outs[1:]
    z = place[0]
    return outs[0], [
        jnp.concatenate(
            [
                lax.dynamic_slice(outs[1], (0, ((z + j) % z_n) * depth), (rank, depth)),
                lax.dynamic_slice(outs[2], (0, ((z + j) % z_n) * up_width), (rank, up_width)),
            ],
            axis=1,
        )
        for j in range(z_n)
    ]


def dots_kernel(z_n, shards, totals, packed, place_ref, tokens_ref, pair_ref, *refs):
    count = sum(len(group) for group in shards)
    unit_refs, refs = refs[:count], refs[count:]
    total_refs, out_refs = refs[:totals], refs[totals : totals + 2 * len(shards)]
    if packed:
        out_refs = [refs[totals].at[n] for n in range(2 * len(shards))]
    if totals == 1:
        total_refs = [total_refs[0].at[n] for n in range(2 * len(shards))]
    buffers, semaphores = refs[-4:-2], refs[-2:]
    depth = unit_refs[0].shape[0]
    only = {d for group in shards for d in group}
    fetches = []
    for side, ref in enumerate((tokens_ref, pair_ref)):
        if len(only) == 1:
            at = pl.multiple_of(((place_ref[0] - min(only) + z_n) % z_n) * depth, 128)
            ref = ref.at[:, pl.ds(at, depth)]
        fetches.append(pltpu.make_async_copy(ref, buffers[side], semaphores[side]))
        fetches[side].start()
    for side in range(2):
        fetches[side].wait()
        n = 0
        for u, group in enumerate(shards):
            value = None
            for d in group:
                at = pl.multiple_of(((place_ref[0] - d + z_n) % z_n) * depth, 128)
                left = (
                    buffers[side][...]
                    if len(only) == 1
                    else buffers[side][:, pl.ds(at, depth)]
                )
                part = jnp.dot(left, unit_refs[n][...], preferred_element_type=jnp.float32)
                value = part if value is None else value + part
                n += 1
            at = side * len(shards) + u
            if totals:
                value = total_refs[at][...] + (0.0 if value is None else value)
            out_refs[at][...] = value


def add_dots(z_n, place, tokens, pair, shards, units, totals, packed=False):
    rows = tokens.shape[0]
    depth, width = next(unit.shape for group in units for unit in group)
    count = len(shards)
    if depth % 128 or width % 128:
        outs = []
        for side, array in enumerate((tokens, pair)):
            for u, group in enumerate(shards):
                at = side * count + u
                value = 0.0 if not totals else totals[0][at] if len(totals) == 1 else totals[at]
                for d, unit in zip(group, units[u]):
                    at = ((place[0] - d) % z_n) * depth
                    value = value + jnp.dot(
                        lax.dynamic_slice(array, (0, at), (rows, depth)),
                        unit,
                        preferred_element_type=jnp.float32,
                    )
                outs.append(value)
        return [jnp.stack(outs)] if packed else outs
    hbm = pl.BlockSpec(memory_space=pltpu.HBM)
    vmem = pl.BlockSpec(memory_space=pltpu.VMEM)
    flat = [unit for group in units for unit in group]
    only = {d for group in shards for d in group}
    buffer = pltpu.VMEM((rows, depth if len(only) == 1 else tokens.shape[1]), tokens.dtype)
    outs = pl.pallas_call(
        functools.partial(dots_kernel, z_n, shards, len(totals), packed),
        in_specs=[pl.BlockSpec(memory_space=pltpu.SMEM), hbm, hbm]
        + [vmem] * (len(flat) + len(totals)),
        out_specs=[vmem] * (1 if packed else 2 * count),
        out_shape=[jax.ShapeDtypeStruct((2 * count, rows, width), jnp.float32)]
        if packed
        else [jax.ShapeDtypeStruct((rows, width), jnp.float32)] * (2 * count),
        scratch_shapes=[buffer, buffer, pltpu.SemaphoreType.DMA, pltpu.SemaphoreType.DMA],
        compiler_params=pltpu.CompilerParams(vmem_limit_bytes=20 * 1024 * 1024),
    )(place, tokens, pair, *flat, *totals)
    return list(outs)


def after(value, *others):
    return lax.optimization_barrier((value,) + others)[0]


def per_device(
    tokens,
    frozen_key_weight,
    key_norm_gain,
    adapter_down_weight,
    adapter_up_weight,
    packed_block_adapter,
    adapter_storage_row,
    live_adapter_rank,
    document_numbers,
    rotated_key_gradient,
):
    rows = tokens.shape[0]
    features = rotated_key_gradient.shape[1]
    depth = frozen_key_weight.shape[0]
    owned, rank, down_width = adapter_down_weight.shape
    up_width = adapter_up_weight.shape[2]
    copies_n = lax.axis_size("copies")
    z_n = lax.axis_size("fsdp")
    group_n = lax.axis_size("adapter")
    x_n = group_n // 2
    y = lax.axis_index("copies")
    z = lax.axis_index("fsdp")
    a = lax.axis_index("adapter")
    x, core = a // 2, a % 2

    def over_core(v):
        return lax.ppermute(v, "adapter", [(i, i ^ 1) for i in range(group_n)])

    def over_x(v, e):
        return lax.ppermute(
            v, "adapter", [(i, ((i // 2 + e) % x_n) * 2 + i % 2) for i in range(group_n)]
        )

    def over_y(v, g):
        return lax.ppermute(v, "copies", [(i, (i + g) % copies_n) for i in range(copies_n)])

    def over_z(v, d):
        return lax.ppermute(v, "fsdp", [(i, (i + d) % z_n) for i in range(z_n)])

    half = features // 2
    units = copies_n * x_n
    unit_width = half // units

    def unit_at(y_at, x_at):
        at = core * half + (y_at * x_n + x_at) * unit_width
        return lax.dynamic_slice(frozen_key_weight, (0, at), (depth, unit_width))

    unit = unit_at(y, x)
    sizes = (x_n, z_n)
    place = jnp.stack([z, a]).astype(jnp.int32)
    numbers = jnp.concatenate([place, packed_block_adapter, adapter_storage_row])
    shifts = sorted(range(1, z_n), key=lambda d: min(d, z_n - d))
    final = len(shifts) - 1

    tokens_pair = over_core(tokens)
    picked = pick_rows(sizes, numbers, adapter_down_weight, adapter_up_weight)
    taken = [over_core(picked[x_n + e]) for e in range(x_n)]
    away = [picked[e] + after(taken[e], tokens_pair, taken[0]) for e in range(1, x_n)]
    slices = picked[0] + taken[0]
    from_z = {d: over_z(unit, d) for d in shifts[:2]}
    for d in shifts[2:]:
        step = 1 if 2 * d <= z_n else z_n - 1
        from_z[d] = over_z(after(from_z[(d - step) % z_n], *away), step)
    for e in range(1, x_n):
        slices = slices + over_x(away[e - 1], e)

    documents, packed, ranks, gain = lax.optimization_barrier(
        (
            document_numbers,
            packed_block_adapter,
            live_adapter_rank,
            key_norm_gain,
            away[0],
        )
    )[:4]
    mine = jnp.arange(packed.shape[0], dtype=jnp.int32) == z * group_n + a
    mine = jnp.arange(ranks.shape[0], dtype=jnp.int32) == jnp.sum(jnp.where(mine, packed, 0))
    live_rank = jnp.sum(jnp.where(mine, ranks, 0)).reshape(1, 1)
    cosine_part, sine_part = rope_tables(doc_positions(documents), key_norm_gain.shape[0])
    cosine = jnp.concatenate([cosine_part, cosine_part], axis=1)
    sine = jnp.concatenate([-sine_part, sine_part], axis=1)

    frozen_key_weight = after(frozen_key_weight, away[0])
    own_units = [
        unit_at((y - g) % copies_n, (x - e) % x_n) for g in range(copies_n) for e in range(x_n)
    ]
    totals = add_dots(
        z_n,
        after(place, cosine, sine, live_rank),
        tokens,
        tokens_pair,
        [[0]] * units,
        [[v] for v in own_units],
        [],
        packed=True,
    )
    along_x, along_y, diagonal = [], [], []
    for k, d in enumerate(shifts):
        gate = away[0] if k < 2 else along_y[k - 2][-1]
        along_y.append([over_y(after(from_z[d], gate), g) for g in range(1, copies_n)])
    for k, d in enumerate(shifts):
        gate = (along_y[0][-1], totals[0], along_y[1][-1])[min(k, 2)]
        along_x.append([over_x(after(from_z[d], gate), e) for e in range(1, x_n)])
    for k, d in enumerate(shifts):
        if k < final:
            gate = along_y[k + 1][-1]
            diagonal.append(
                [[over_y(after(v, gate), g) for v in along_x[k]] for g in range(1, copies_n)]
            )
    diagonal.append(
        [
            [over_x(after(v, along_x[max(final - 1, 0)][-1]), e) for e in range(1, x_n)]
            for v in along_y[final]
        ]
    )
    shards = {}
    for k, d in enumerate(shifts):
        shards[d] = [from_z[d]] + along_x[k]
        for g in range(1, copies_n):
            shards[d] += [along_y[k][g - 1]] + diagonal[k][g - 1]
    early, late = [], []
    for u in range(units):
        g, e = u // x_n, u % x_n
        early.append([d for d in shifts if not (g and e) and not (e and d == shifts[final])])
        late.append([d for d in shifts if d not in early[u]])
    totals = add_dots(
        z_n,
        place,
        tokens,
        tokens_pair,
        early,
        [[shards[d][u] for d in group] for u, group in enumerate(early)],
        totals,
    )
    adapter_slices = {0: slices[0]}
    for k, d in enumerate(shifts):
        gates = ()
        adapter_slices[(-d) % z_n] = over_z(after(slices[d], *gates), d)
    open_units = [u for u in range(units) if late[u]]
    done = add_dots(
        z_n,
        after(place, *adapter_slices.values()),
        tokens,
        tokens_pair,
        [late[u] for u in open_units],
        [[shards[d][u] for d in late[u]] for u in open_units],
        [totals[u] for u in open_units] + [totals[units + u] for u in open_units],
    )
    bases = list(totals)
    for n, u in enumerate(open_units):
        bases[u], bases[units + u] = done[n], done[len(open_units) + n]
    bases = bases[:units] + [over_core(v) for v in bases[units:]]
    head = key_norm_gain.shape[0]
    columns = [
        (((y - g) % copies_n) * x_n + (x - e) % x_n) * unit_width
        for g in range(copies_n)
        for e in range(x_n)
    ]
    if unit_width % head:
        natural = []
        for side in (bases[:units], bases[units:]):
            stack = jnp.stack(side)
            order = jnp.stack(
                [
                    ((y - y_at) % copies_n) * x_n + (x - x_at) % x_n
                    for y_at in range(copies_n)
                    for x_at in range(x_n)
                ]
            )
            whole = jnp.swapaxes(stack[order], 0, 1).reshape(rows, half)
            natural.append(whole)
        bases = natural
        columns = [jnp.zeros_like(z)]

    low, up, update = low_and_update(
        z_n,
        place,
        live_rank,
        tokens,
        [adapter_slices[j] for j in range(z_n)],
    )
    rotated, sent = norm_and_back(
        z_n,
        place,
        jnp.stack(columns).astype(jnp.int32),
        live_rank,
        bases,
        update,
        low,
        up,
        cosine,
        sine,
        gain[None],
        rotated_key_gradient,
        tokens,
    )
    order = [0] + shifts if z_n <= 4 else list(range(z_n))
    step = -(-z_n // 4)
    groups = [tuple(order[k : k + step]) for k in range(0, z_n, step)]
    arrived = {d: sent[0] if d == 0 else over_z(sent[d], d) for d in order}
    blocks = []
    for group in groups:
        if len(group) == 1:
            here = arrived[group[0]][None]
        else:
            here = jnp.stack([arrived[d] for d in group])
        for e in range(x_n):
            there = over_x(here, e) if e else here
            blocks += [there, over_core(there)]
    grad_down, grad_up = owner_sum(
        sizes,
        groups,
        numbers,
        blocks,
        owned,
        down_width,
    )
    return (rotated, grad_down, grad_up)


def solution(mesh):
    return jax.shard_map(
        per_device,
        mesh=mesh,
        in_specs=(
            P(("copies", "fsdp", "adapter"), None),
            P("fsdp", None),
            P(),
            P("adapter", None, "fsdp"),
            P("adapter", None, "fsdp"),
            P("copies"),
            P(),
            P(),
            P(("copies", "fsdp", "adapter")),
            P(("copies", "fsdp", "adapter"), None),
        ),
        out_specs=(
            P(("copies", "fsdp", "adapter"), None),
            P(("copies", "adapter"), None, "fsdp"),
            P(("copies", "adapter"), None, "fsdp"),
        ),
        check_vma=False,
    )
```

```python
import functools

import jax
import jax.numpy as jnp
from jax import lax
from jax.experimental import pallas as pl
from jax.experimental.pallas import tpu as pltpu
from jax.sharding import PartitionSpec as P

BLOCK_LENGTH = 256
ADAPTER_STRENGTH = 16.0
ROPE_BASE = 1000000.0


def rope_tables(positions, head_size):
    half_head = head_size // 2
    steps_iota = jnp.arange(half_head, dtype=jnp.float32)
    frequency = jnp.exp(-jnp.log(jnp.float32(ROPE_BASE)) * 2.0 * steps_iota / head_size)
    angles = positions.astype(jnp.float32)[:, None] * frequency[None, :]
    return (jnp.cos(angles), jnp.sin(angles))


def doc_positions(document_numbers):
    count = document_numbers.shape[0]
    index_iota = jnp.arange(count, dtype=jnp.int32)
    previous = jnp.concatenate([document_numbers[:1], document_numbers[:-1]])
    doc_start = jnp.logical_or(index_iota % BLOCK_LENGTH == 0, document_numbers != previous)
    first_index = lax.cummax(jnp.where(doc_start, index_iota, 0), axis=0)
    return index_iota - first_index


def block_row(numbers, blocks, z_to, group_to, group_n):
    return numbers[2 + blocks + numbers[2 + z_to * group_n + group_to]]


def pick_kernel(sizes, numbers, down_ref, up_ref, *refs):
    x_n, z_n = sizes
    out_refs, (down_buffer, up_buffer, semaphores) = refs[: 2 * x_n], refs[2 * x_n :]
    owned = down_ref.shape[0]
    z, a = numbers[0], numbers[1]
    x, core = a // 2, a % 2

    def for_block(n, act):
        pair, e, j = n // (x_n * z_n), n // z_n % x_n, n % z_n
        group_to = ((x + e) % x_n) * 2 + (core + pair) % 2
        row = block_row(numbers, 2 * x_n * z_n, (z + j) % z_n, group_to, 2 * x_n) - a * owned
        hit = jnp.logical_and(row >= 0, row < owned)

        @pl.when(hit)
        def _():
            act(pltpu.make_async_copy(down_ref.at[row], down_buffer.at[n], semaphores.at[0, n]))
            act(pltpu.make_async_copy(up_ref.at[row], up_buffer.at[n], semaphores.at[1, n]))

        return hit

    def start(n, carry):
        for_block(n, lambda copy: copy.start())
        return carry

    lax.fori_loop(0, 2 * x_n * z_n, start, 0)
    for m in range(2 * x_n):

        def finish(j, carry, m=m):
            n = m * z_n + j
            hit = for_block(n, lambda copy: copy.wait())

            @pl.when(hit)
            def _():
                out_refs[m][j] = jnp.concatenate([down_buffer[n], up_buffer[n]], axis=1)

            @pl.when(jnp.logical_not(hit))
            def _():
                out_refs[m][j] = jnp.zeros_like(out_refs[m][j])

            return carry

        lax.fori_loop(0, z_n, finish, 0)


def pick_rows(sizes, numbers, down, up):
    x_n, z_n = sizes
    count = 2 * x_n * z_n
    _, rank, down_width = down.shape
    up_width = up.shape[2]
    return pl.pallas_call(
        functools.partial(pick_kernel, sizes),
        in_specs=[pl.BlockSpec(memory_space=pltpu.SMEM)]
        + [pl.BlockSpec(memory_space=pltpu.HBM)] * 2,
        out_specs=[pl.BlockSpec(memory_space=pltpu.VMEM)] * (2 * x_n),
        out_shape=[jax.ShapeDtypeStruct((z_n, rank, down_width + up_width), down.dtype)]
        * (2 * x_n),
        scratch_shapes=[
            pltpu.VMEM((count, rank, down_width), down.dtype),
            pltpu.VMEM((count, rank, up_width), down.dtype),
            pltpu.SemaphoreType.DMA((2, count)),
        ],
        compiler_params=pltpu.CompilerParams(vmem_limit_bytes=56 * 1024 * 1024),
    )(numbers, down, up)


def owner_sum_kernel(sizes, groups, numbers, *refs):
    x_n, z_n = sizes
    count = x_n * 2 * len(groups)
    block_refs, down_ref, up_ref = refs[:count], refs[count], refs[count + 1]
    owned, tile, down_width = down_ref.shape
    first_row = pl.multiple_of(pl.program_id(0) * tile, tile)
    z, a = numbers[0], numbers[1]
    x, core = a // 2, a % 2
    down_ref[...] = jnp.zeros_like(down_ref)
    up_ref[...] = jnp.zeros_like(up_ref)
    i = 0
    for group in groups:
        for e in range(x_n):
            for pair in range(2):
                group_from = ((x - e + x_n) % x_n) * 2 + (core + pair) % 2

                def one(k, carry, i=i, first=group[0], group_from=group_from):
                    z_from = (z - first - k + z_n) % z_n
                    row = block_row(numbers, 2 * x_n * z_n, z_from, group_from, 2 * x_n)
                    row = row - a * owned

                    @pl.when(jnp.logical_and(row >= 0, row < owned))
                    def _():
                        block = block_refs[i][k, pl.ds(first_row, tile), :].astype(jnp.float32)
                        down_ref[row] += block[:, :down_width]
                        up_ref[row] += block[:, down_width:]

                    return carry

                if len(group) == 1:
                    one(0, 0)
                else:
                    lax.fori_loop(0, len(group), one, 0)
                i += 1


def owner_sum(sizes, groups, numbers, blocks, owned, down_width):
    _, rank, width = blocks[0].shape
    tile = 32
    smem = pl.BlockSpec(memory_space=pltpu.SMEM)
    return pl.pallas_call(
        functools.partial(owner_sum_kernel, sizes, groups),
        grid=(rank // tile,),
        in_specs=[smem]
        + [pl.BlockSpec(memory_space=pltpu.VMEM)] * len(blocks),
        out_specs=[
            pl.BlockSpec((owned, tile, down_width), lambda t: (0, t, 0)),
            pl.BlockSpec((owned, tile, width - down_width), lambda t: (0, t, 0)),
        ],
        out_shape=[
            jax.ShapeDtypeStruct((owned, rank, down_width), jnp.float32),
            jax.ShapeDtypeStruct((owned, rank, width - down_width), jnp.float32),
        ],
        compiler_params=pltpu.CompilerParams(vmem_limit_bytes=24 * 1024 * 1024),
    )(numbers, *blocks)


def low_kernel(
    z_n, place_ref, rank_ref, tokens_ref, *refs,
):
    slice_refs = refs[:z_n]
    low_ref, up_ref, update_ref, tokens_buffer, semaphore = refs[z_n:]
    fetch = pltpu.make_async_copy(tokens_ref, tokens_buffer, semaphore)
    fetch.start()
    z = place_ref[0]
    rank, depth = low_ref.shape[1], tokens_ref.shape[1] // z_n
    up_width = up_ref.shape[1] // z_n
    for j in range(z_n):
        f = (z + j) % z_n
        up_ref[:, pl.ds(pl.multiple_of(f * up_width, 128), up_width)] = slice_refs[j][:, depth:]
    fetch.wait()
    low = None
    for j in range(z_n):
        f = (z + j) % z_n
        part = lax.dot_general(
            tokens_buffer[:, pl.ds(pl.multiple_of(f * depth, 128), depth)],
            slice_refs[j][:, :depth],
            (((1,), (1,)), ((), ())),
            preferred_element_type=jnp.float32,
        )
        low = part if low is None else low + part
    live = lax.broadcasted_iota(jnp.int32, (1, rank), 1) < rank_ref[...]
    low = jnp.where(live, low, 0.0).astype(jnp.bfloat16)
    low_ref[...] = low
    scale = ADAPTER_STRENGTH / rank_ref[...].astype(jnp.float32)
    update_ref[...] = scale * jnp.dot(
        low, up_ref[...], preferred_element_type=jnp.float32
    )


def low_and_update(z_n, place, live_rank, tokens, slices):
    rows, width = tokens.shape
    rank, slice_width = slices[0].shape
    depth = width // z_n
    up_width = slice_width - depth
    features = up_width * z_n
    smem = pl.BlockSpec(memory_space=pltpu.SMEM)
    vmem = pl.BlockSpec(memory_space=pltpu.VMEM)
    if depth % 128 == 0 and up_width % 128 == 0:
        return pl.pallas_call(
            functools.partial(low_kernel, z_n),
            in_specs=[smem, vmem, pl.BlockSpec(memory_space=pltpu.HBM)] + [vmem] * z_n,
            out_specs=[vmem] * 3,
            out_shape=[
                jax.ShapeDtypeStruct((rows, rank), jnp.bfloat16),
                jax.ShapeDtypeStruct((rank, features), jnp.bfloat16),
                jax.ShapeDtypeStruct((rows, features), jnp.float32),
            ],
            scratch_shapes=[pltpu.VMEM((rows, width), tokens.dtype), pltpu.SemaphoreType.DMA],
            compiler_params=pltpu.CompilerParams(vmem_limit_bytes=16 * 1024 * 1024),
        )(place, live_rank, tokens, *slices)
    z = place[0]
    stack = jnp.stack(slices)[(jnp.arange(z_n) - z) % z_n]
    down = jnp.swapaxes(stack[:, :, :depth], 0, 1).reshape(rank, width)
    up = jnp.swapaxes(stack[:, :, depth:], 0, 1).reshape(rank, features)
    low = lax.dot_general(
        tokens, down, (((1,), (1,)), ((), ())), preferred_element_type=jnp.float32
    )
    live = jnp.arange(rank, dtype=jnp.int32)[None, :] < live_rank
    low = jnp.where(live, low, 0.0).astype(jnp.bfloat16)
    scale = ADAPTER_STRENGTH / live_rank.astype(jnp.float32)
    return low, up, scale * jnp.dot(low, up, preferred_element_type=jnp.float32)


def norm_kernel(
    z_n, units, place_ref, columns_ref, rank_ref, *refs,
):
    base_refs, refs = refs[: 2 * units], refs[2 * units :]
    update_ref, low_ref, up_ref, cosine_ref, sine_ref, gain_ref = refs[:6]
    gradient_ref, tokens_ref, keys_ref = refs[6:9]
    refs = refs[9:]
    sent_refs, (tokens_buffer, gradient_buffer, part_up, semaphores) = refs[:-4], refs[-4:]
    fetch_gradient = pltpu.make_async_copy(gradient_ref, gradient_buffer, semaphores.at[0])
    fetch_tokens = pltpu.make_async_copy(tokens_ref, tokens_buffer, semaphores.at[1])
    fetch_gradient.start()
    fetch_tokens.start()
    z, core = place_ref[0], place_ref[1] % 2
    scale = ADAPTER_STRENGTH / rank_ref[...].astype(jnp.float32)
    head = gain_ref.shape[1]
    width = base_refs[0].shape[1]
    half = units * width
    low = low_ref[...]
    cosine, sine, gain = cosine_ref[...], sine_ref[...], gain_ref[...]
    gain_cosine, gain_sine = cosine * gain, sine * pltpu.roll(gain, head // 2, 1)
    grad_low = None
    fetch_gradient.wait()
    for n, base_ref in enumerate(base_refs):
        first = (core if n < units else 1 - core) * half + columns_ref[n % units]
        for i in range(width // head):
            at = pl.ds(pl.multiple_of(first + i * head, 128), head)
            up = up_ref[:, at]
            pre = base_ref[:, i * head : (i + 1) * head] + update_ref[:, at]
            inverse = lax.rsqrt(jnp.mean(pre * pre, axis=1, keepdims=True) + 1e-06)
            unit = pre * inverse
            keys = unit * gain_cosine + pltpu.roll(unit, head // 2, 1) * gain_sine
            keys_ref[:, at] = keys.astype(keys_ref.dtype)
            gradient = gradient_buffer[:, at].astype(jnp.float32)
            turned = gain * (gradient * cosine - pltpu.roll(gradient, head // 2, 1) * sine)
            along = jnp.mean(turned * unit, axis=1, keepdims=True)
            scaled = ((scale * inverse) * (turned - unit * along)).astype(jnp.bfloat16)
            part_low = lax.dot_general(
                scaled, up, (((1,), (1,)), ((), ())), preferred_element_type=jnp.float32
            )
            grad_low = part_low if grad_low is None else grad_low + part_low
            part_up[:, at] = lax.dot_general(
                low, scaled, (((0,), (0,)), ((), ())), preferred_element_type=jnp.float32
            ).astype(part_up.dtype)
    live = lax.broadcasted_iota(jnp.int32, (1, low.shape[1]), 1) < rank_ref[...]
    grad_low = jnp.where(live, grad_low, 0.0).astype(jnp.bfloat16)
    fetch_tokens.wait()
    if len(sent_refs) == 2:
        sent_refs[0][...] = lax.dot_general(
            grad_low, tokens_buffer[...], (((0,), (0,)), ((), ())),
            preferred_element_type=jnp.float32,
        ).astype(jnp.bfloat16)
        sent_refs[1][...] = part_up[...]
        return
    depth = tokens_ref.shape[1] // z_n
    up_width = part_up.shape[1] // z_n
    for j in range(z_n):
        f = (z + j) % z_n
        sent_refs[j][:, :depth] = lax.dot_general(
            grad_low,
            tokens_buffer[:, pl.ds(pl.multiple_of(f * depth, 128), depth)],
            (((0,), (0,)), ((), ())),
            preferred_element_type=jnp.float32,
        ).astype(jnp.bfloat16)
        sent_refs[j][:, depth:] = part_up[:, pl.ds(pl.multiple_of(f * up_width, 128), up_width)]


def norm_and_back(
    z_n, place, columns, live_rank, bases, update, low, up, cosine, sine, gain,
    gradient, tokens,
):
    rows, features = gradient.shape
    rank = up.shape[0]
    width = tokens.shape[1]
    depth, up_width = width // z_n, features // z_n
    aligned = depth % 128 == 0 and up_width % 128 == 0
    if aligned:
        sent = [jax.ShapeDtypeStruct((rank, depth + up_width), jnp.bfloat16)] * z_n
    else:
        sent = [
            jax.ShapeDtypeStruct((rank, width), jnp.bfloat16),
            jax.ShapeDtypeStruct((rank, features), jnp.bfloat16),
        ]
    smem = pl.BlockSpec(memory_space=pltpu.SMEM)
    vmem = pl.BlockSpec(memory_space=pltpu.VMEM)
    hbm = pl.BlockSpec(memory_space=pltpu.HBM)
    outs = pl.pallas_call(
        functools.partial(norm_kernel, z_n, len(bases) // 2),
        in_specs=[smem] * 2 + [vmem] * (len(bases) + 7) + [hbm] * 2,
        out_specs=[vmem] * (1 + len(sent)),
        out_shape=[jax.ShapeDtypeStruct((rows, features), jnp.bfloat16)] + sent,
        scratch_shapes=[
            pltpu.VMEM((rows, width), tokens.dtype),
            pltpu.VMEM((rows, features), gradient.dtype),
            pltpu.VMEM((rank, features), jnp.bfloat16),
            pltpu.SemaphoreType.DMA((2,)),
        ],
        compiler_params=pltpu.CompilerParams(vmem_limit_bytes=24 * 1024 * 1024),
    )(
        place, columns, live_rank, *bases, update, low, up, cosine, sine, gain,
        gradient, tokens,
    )
    if aligned:
        return outs[0], outs[1:]
    z = place[0]
    return outs[0], [
        jnp.concatenate(
            [
                lax.dynamic_slice(outs[1], (0, ((z + j) % z_n) * depth), (rank, depth)),
                lax.dynamic_slice(outs[2], (0, ((z + j) % z_n) * up_width), (rank, up_width)),
            ],
            axis=1,
        )
        for j in range(z_n)
    ]


def dots_kernel(z_n, shards, totals, packed, place_ref, tokens_ref, pair_ref, *refs):
    count = sum(len(group) for group in shards)
    unit_refs, refs = refs[:count], refs[count:]
    total_refs, out_refs = refs[:totals], refs[totals : totals + 2 * len(shards)]
    if packed:
        out_refs = [refs[totals].at[n] for n in range(2 * len(shards))]
    if totals == 1:
        total_refs = [total_refs[0].at[n] for n in range(2 * len(shards))]
    depth = unit_refs[0].shape[0]
    for side, ref in enumerate((tokens_ref, pair_ref)):
        n = 0
        for u, group in enumerate(shards):
            value = None
            for d in group:
                at = pl.multiple_of(((place_ref[0] - d + z_n) % z_n) * depth, 128)
                left = ref[:, pl.ds(at, depth)]
                part = jnp.dot(left, unit_refs[n][...], preferred_element_type=jnp.float32)
                value = part if value is None else value + part
                n += 1
            at = side * len(shards) + u
            if totals:
                value = total_refs[at][...] + (0.0 if value is None else value)
            out_refs[at][...] = value


def add_dots(z_n, place, tokens, pair, shards, units, totals, packed=False):
    rows = tokens.shape[0]
    depth, width = next(unit.shape for group in units for unit in group)
    count = len(shards)
    if depth % 128 or width % 128:
        outs = []
        for side, array in enumerate((tokens, pair)):
            for u, group in enumerate(shards):
                at = side * count + u
                value = 0.0 if not totals else totals[0][at] if len(totals) == 1 else totals[at]
                for d, unit in zip(group, units[u]):
                    at = ((place[0] - d) % z_n) * depth
                    value = value + jnp.dot(
                        lax.dynamic_slice(array, (0, at), (rows, depth)),
                        unit,
                        preferred_element_type=jnp.float32,
                    )
                outs.append(value)
        return [jnp.stack(outs)] if packed else outs
    vmem = pl.BlockSpec(memory_space=pltpu.VMEM)
    flat = [unit for group in units for unit in group]
    outs = pl.pallas_call(
        functools.partial(dots_kernel, z_n, shards, len(totals), packed),
        in_specs=[pl.BlockSpec(memory_space=pltpu.SMEM)] + [vmem] * (2 + len(flat) + len(totals)),
        out_specs=[vmem] * (1 if packed else 2 * count),
        out_shape=[jax.ShapeDtypeStruct((2 * count, rows, width), jnp.float32)]
        if packed
        else [jax.ShapeDtypeStruct((rows, width), jnp.float32)] * (2 * count),
        compiler_params=pltpu.CompilerParams(vmem_limit_bytes=20 * 1024 * 1024),
    )(place, tokens, pair, *flat, *totals)
    return list(outs)


def after(value, *others):
    return lax.optimization_barrier((value,) + others)[0]


def per_device(
    tokens,
    frozen_key_weight,
    key_norm_gain,
    adapter_down_weight,
    adapter_up_weight,
    packed_block_adapter,
    adapter_storage_row,
    live_adapter_rank,
    document_numbers,
    rotated_key_gradient,
):
    rows = tokens.shape[0]
    features = rotated_key_gradient.shape[1]
    depth = frozen_key_weight.shape[0]
    owned, rank, down_width = adapter_down_weight.shape
    up_width = adapter_up_weight.shape[2]
    copies_n = lax.axis_size("copies")
    z_n = lax.axis_size("fsdp")
    group_n = lax.axis_size("adapter")
    x_n = group_n // 2
    y = lax.axis_index("copies")
    z = lax.axis_index("fsdp")
    a = lax.axis_index("adapter")
    x, core = a // 2, a % 2

    def over_core(v):
        return lax.ppermute(v, "adapter", [(i, i ^ 1) for i in range(group_n)])

    def over_x(v, e):
        return lax.ppermute(
            v, "adapter", [(i, ((i // 2 + e) % x_n) * 2 + i % 2) for i in range(group_n)]
        )

    def over_y(v, g):
        return lax.ppermute(v, "copies", [(i, (i + g) % copies_n) for i in range(copies_n)])

    def over_z(v, d):
        return lax.ppermute(v, "fsdp", [(i, (i + d) % z_n) for i in range(z_n)])

    half = features // 2
    units = copies_n * x_n
    unit_width = half // units

    def unit_at(y_at, x_at):
        at = core * half + (y_at * x_n + x_at) * unit_width
        return lax.dynamic_slice(frozen_key_weight, (0, at), (depth, unit_width))

    unit = unit_at(y, x)
    sizes = (x_n, z_n)
    place = jnp.stack([z, a]).astype(jnp.int32)
    numbers = jnp.concatenate([place, packed_block_adapter, adapter_storage_row])
    shifts = sorted(range(1, z_n), key=lambda d: min(d, z_n - d))
    final = len(shifts) - 1

    tokens_pair = over_core(tokens)
    picked = pick_rows(sizes, numbers, adapter_down_weight, adapter_up_weight)
    taken = [over_core(picked[x_n + e]) for e in range(x_n)]
    away = [picked[e] + after(taken[e], tokens_pair, taken[0]) for e in range(1, x_n)]
    slices = picked[0] + taken[0]
    from_z = {d: over_z(unit, d) for d in shifts[:2]}
    for d in shifts[2:]:
        step = 1 if 2 * d <= z_n else z_n - 1
        from_z[d] = over_z(after(from_z[(d - step) % z_n], *away), step)
    for e in range(1, x_n):
        slices = slices + over_x(away[e - 1], e)

    documents, packed, ranks, gain = lax.optimization_barrier(
        (
            document_numbers,
            packed_block_adapter,
            live_adapter_rank,
            key_norm_gain,
            away[0],
        )
    )[:4]
    mine = jnp.arange(packed.shape[0], dtype=jnp.int32) == z * group_n + a
    mine = jnp.arange(ranks.shape[0], dtype=jnp.int32) == jnp.sum(jnp.where(mine, packed, 0))
    live_rank = jnp.sum(jnp.where(mine, ranks, 0)).reshape(1, 1)
    cosine_part, sine_part = rope_tables(doc_positions(documents), key_norm_gain.shape[0])
    cosine = jnp.concatenate([cosine_part, cosine_part], axis=1)
    sine = jnp.concatenate([-sine_part, sine_part], axis=1)

    frozen_key_weight = after(frozen_key_weight, away[0])
    own_units = [
        unit_at((y - g) % copies_n, (x - e) % x_n) for g in range(copies_n) for e in range(x_n)
    ]
    totals = add_dots(
        z_n,
        after(place, cosine, sine, live_rank),
        tokens,
        tokens_pair,
        [[0]] * units,
        [[v] for v in own_units],
        [],
        packed=True,
    )
    along_x, along_y, diagonal = [], [], []
    for k, d in enumerate(shifts):
        gate = away[0] if k < 2 else along_y[k - 2][-1]
        along_y.append([over_y(after(from_z[d], gate), g) for g in range(1, copies_n)])
    for k, d in enumerate(shifts):
        gate = (along_y[0][-1], totals[0], along_y[1][-1])[min(k, 2)]
        along_x.append([over_x(after(from_z[d], gate), e) for e in range(1, x_n)])
    for k, d in enumerate(shifts):
        if k < final:
            gate = along_y[k + 1][-1]
            diagonal.append(
                [[over_y(after(v, gate), g) for v in along_x[k]] for g in range(1, copies_n)]
            )
    diagonal.append(
        [
            [over_x(after(v, along_x[max(final - 1, 0)][-1]), e) for e in range(1, x_n)]
            for v in along_y[final]
        ]
    )
    shards = {}
    for k, d in enumerate(shifts):
        shards[d] = [from_z[d]] + along_x[k]
        for g in range(1, copies_n):
            shards[d] += [along_y[k][g - 1]] + diagonal[k][g - 1]
    early, late = [], []
    for u in range(units):
        g, e = u // x_n, u % x_n
        early.append([d for d in shifts if not (g and e) and not (e and d == shifts[final])])
        late.append([d for d in shifts if d not in early[u]])
    totals = add_dots(
        z_n,
        place,
        tokens,
        tokens_pair,
        early,
        [[shards[d][u] for d in group] for u, group in enumerate(early)],
        totals,
    )
    adapter_slices = {0: slices[0]}
    for k, d in enumerate(shifts):
        gates = ()
        adapter_slices[(-d) % z_n] = over_z(after(slices[d], *gates), d)
    low, up, update = low_and_update(
        z_n,
        place,
        live_rank,
        tokens,
        [adapter_slices[j] for j in range(z_n)],
    )
    open_units = [u for u in range(units) if late[u]]
    done = add_dots(
        z_n,
        after(place, low),
        tokens,
        tokens_pair,
        [late[u] for u in open_units],
        [[shards[d][u] for d in late[u]] for u in open_units],
        [totals[u] for u in open_units] + [totals[units + u] for u in open_units],
    )
    bases = list(totals)
    for n, u in enumerate(open_units):
        bases[u], bases[units + u] = done[n], done[len(open_units) + n]
    bases = bases[:units] + [over_core(v) for v in bases[units:]]
    head = key_norm_gain.shape[0]
    columns = [
        (((y - g) % copies_n) * x_n + (x - e) % x_n) * unit_width
        for g in range(copies_n)
        for e in range(x_n)
    ]
    if unit_width % head:
        natural = []
        for side in (bases[:units], bases[units:]):
            stack = jnp.stack(side)
            order = jnp.stack(
                [
                    ((y - y_at) % copies_n) * x_n + (x - x_at) % x_n
                    for y_at in range(copies_n)
                    for x_at in range(x_n)
                ]
            )
            whole = jnp.swapaxes(stack[order], 0, 1).reshape(rows, half)
            natural.append(whole)
        bases = natural
        columns = [jnp.zeros_like(z)]

    rotated, sent = norm_and_back(
        z_n,
        place,
        jnp.stack(columns).astype(jnp.int32),
        live_rank,
        bases,
        update,
        low,
        up,
        cosine,
        sine,
        gain[None],
        rotated_key_gradient,
        tokens,
    )
    order = [0] + shifts if z_n <= 4 else list(range(z_n))
    step = -(-z_n // 4)
    groups = [tuple(order[k : k + step]) for k in range(0, z_n, step)]
    arrived = {d: sent[0] if d == 0 else over_z(sent[d], d) for d in order}
    blocks = []
    for group in groups:
        if len(group) == 1:
            here = arrived[group[0]][None]
        else:
            here = jnp.stack([arrived[d] for d in group])
        for e in range(x_n):
            there = over_x(here, e) if e else here
            blocks += [there, over_core(there)]
    grad_down, grad_up = owner_sum(
        sizes,
        groups,
        numbers,
        blocks,
        owned,
        down_width,
    )
    return (rotated, grad_down, grad_up)


def solution(mesh):
    return jax.shard_map(
        per_device,
        mesh=mesh,
        in_specs=(
            P(("copies", "fsdp", "adapter"), None),
            P("fsdp", None),
            P(),
            P("adapter", None, "fsdp"),
            P("adapter", None, "fsdp"),
            P("copies"),
            P(),
            P(),
            P(("copies", "fsdp", "adapter")),
            P(("copies", "fsdp", "adapter"), None),
        ),
        out_specs=(
            P(("copies", "fsdp", "adapter"), None),
            P(("copies", "adapter"), None, "fsdp"),
            P(("copies", "adapter"), None, "fsdp"),
        ),
        check_vma=False,
    )
```

```python
import functools

import jax
import jax.numpy as jnp
from jax import lax
from jax.experimental import pallas as pl
from jax.experimental.pallas import tpu as pltpu
from jax.sharding import PartitionSpec as P

BLOCK_LENGTH = 256
ADAPTER_STRENGTH = 16.0
ROPE_BASE = 1000000.0


def rope_tables(positions, head_size):
    half_head = head_size // 2
    steps_iota = jnp.arange(half_head, dtype=jnp.float32)
    frequency = jnp.exp(-jnp.log(jnp.float32(ROPE_BASE)) * 2.0 * steps_iota / head_size)
    angles = positions.astype(jnp.float32)[:, None] * frequency[None, :]
    return (jnp.cos(angles), jnp.sin(angles))


def doc_positions(document_numbers):
    count = document_numbers.shape[0]
    index_iota = jnp.arange(count, dtype=jnp.int32)
    previous = jnp.concatenate([document_numbers[:1], document_numbers[:-1]])
    doc_start = jnp.logical_or(index_iota % BLOCK_LENGTH == 0, document_numbers != previous)
    first_index = lax.cummax(jnp.where(doc_start, index_iota, 0), axis=0)
    return index_iota - first_index


def block_row(packed, storage, z_to, group_to, group_n):
    return storage[packed[z_to * group_n + group_to]]


def pick_kernel(sizes, packed, storage, down_ref, up_ref, *refs):
    x_n, z_n = sizes
    out_refs, (down_buffer, up_buffer, semaphores) = refs[: 2 * x_n], refs[2 * x_n :]
    owned = down_ref.shape[0]
    z, a = lax.axis_index("fsdp"), lax.axis_index("adapter")
    x, core = a // 2, a % 2

    def for_block(n, act):
        pair, e, j = n // (x_n * z_n), n // z_n % x_n, n % z_n
        group_to = ((x + e) % x_n) * 2 + (core + pair) % 2
        row = block_row(packed, storage, (z + j) % z_n, group_to, 2 * x_n) - a * owned
        hit = jnp.logical_and(row >= 0, row < owned)

        @pl.when(hit)
        def _():
            act(pltpu.make_async_copy(down_ref.at[row], down_buffer.at[n], semaphores.at[0, n]))
            act(pltpu.make_async_copy(up_ref.at[row], up_buffer.at[n], semaphores.at[1, n]))

        return hit

    def start(n, carry):
        for_block(n, lambda copy: copy.start())
        return carry

    lax.fori_loop(0, 2 * x_n * z_n, start, 0)
    for m in range(2 * x_n):

        def finish(j, carry, m=m):
            n = m * z_n + j
            hit = for_block(n, lambda copy: copy.wait())

            @pl.when(hit)
            def _():
                out_refs[m][j] = jnp.concatenate([down_buffer[n], up_buffer[n]], axis=1)

            @pl.when(jnp.logical_not(hit))
            def _():
                out_refs[m][j] = jnp.zeros_like(out_refs[m][j])

            return carry

        lax.fori_loop(0, z_n, finish, 0)


def pick_rows(sizes, packed, storage, down, up):
    x_n, z_n = sizes
    count = 2 * x_n * z_n
    _, rank, down_width = down.shape
    up_width = up.shape[2]
    return pl.pallas_call(
        functools.partial(pick_kernel, sizes),
        in_specs=[pl.BlockSpec(memory_space=pltpu.SMEM)] * 2
        + [pl.BlockSpec(memory_space=pltpu.HBM)] * 2,
        out_specs=[pl.BlockSpec(memory_space=pltpu.VMEM)] * (2 * x_n),
        out_shape=[jax.ShapeDtypeStruct((z_n, rank, down_width + up_width), down.dtype)]
        * (2 * x_n),
        scratch_shapes=[
            pltpu.VMEM((count, rank, down_width), down.dtype),
            pltpu.VMEM((count, rank, up_width), down.dtype),
            pltpu.SemaphoreType.DMA((2, count)),
        ],
        compiler_params=pltpu.CompilerParams(vmem_limit_bytes=56 * 1024 * 1024),
    )(packed, storage, down, up)


def owner_sum_kernel(sizes, groups, packed, storage, *refs):
    x_n, z_n = sizes
    count = x_n * 2 * len(groups)
    block_refs, down_ref, up_ref = refs[:count], refs[count], refs[count + 1]
    owned, tile, down_width = down_ref.shape
    first_row = pl.multiple_of(pl.program_id(0) * tile, tile)
    z, a = lax.axis_index("fsdp"), lax.axis_index("adapter")
    x, core = a // 2, a % 2
    down_ref[...] = jnp.zeros_like(down_ref)
    up_ref[...] = jnp.zeros_like(up_ref)
    i = 0
    for group in groups:
        for e in range(x_n):
            for pair in range(2):
                group_from = ((x - e + x_n) % x_n) * 2 + (core + pair) % 2

                def one(k, carry, i=i, first=group[0], group_from=group_from):
                    z_from = (z - first - k + z_n) % z_n
                    row = block_row(packed, storage, z_from, group_from, 2 * x_n)
                    row = row - a * owned

                    @pl.when(jnp.logical_and(row >= 0, row < owned))
                    def _():
                        block = block_refs[i][k, pl.ds(first_row, tile), :].astype(jnp.float32)
                        down_ref[row] += block[:, :down_width]
                        up_ref[row] += block[:, down_width:]

                    return carry

                if len(group) == 1:
                    one(0, 0)
                else:
                    lax.fori_loop(0, len(group), one, 0)
                i += 1


def owner_sum(sizes, groups, packed, storage, blocks, owned, down_width):
    _, rank, width = blocks[0].shape
    tile = 32
    smem = pl.BlockSpec(memory_space=pltpu.SMEM)
    return pl.pallas_call(
        functools.partial(owner_sum_kernel, sizes, groups),
        grid=(rank // tile,),
        in_specs=[smem] * 2 + [pl.BlockSpec(memory_space=pltpu.VMEM)] * len(blocks),
        out_specs=[
            pl.BlockSpec((owned, tile, down_width), lambda t: (0, t, 0)),
            pl.BlockSpec((owned, tile, width - down_width), lambda t: (0, t, 0)),
        ],
        out_shape=[
            jax.ShapeDtypeStruct((owned, rank, down_width), jnp.float32),
            jax.ShapeDtypeStruct((owned, rank, width - down_width), jnp.float32),
        ],
        compiler_params=pltpu.CompilerParams(vmem_limit_bytes=16 * 1024 * 1024),
    )(packed, storage, *blocks)


def low_kernel(
    z_n, place_ref, rank_ref, tokens_ref, *refs,
):
    slice_refs = refs[:z_n]
    low_ref, up_ref, update_ref, tokens_buffer, semaphore = refs[z_n:]
    fetch = pltpu.make_async_copy(tokens_ref, tokens_buffer, semaphore)
    fetch.start()
    z = place_ref[0]
    rank, depth = low_ref.shape[1], tokens_ref.shape[1] // z_n
    up_width = up_ref.shape[1] // z_n
    for j in range(z_n):
        f = (z + j) % z_n
        up_ref[:, pl.ds(pl.multiple_of(f * up_width, 128), up_width)] = slice_refs[j][:, depth:]
    fetch.wait()
    low = None
    for j in range(z_n):
        f = (z + j) % z_n
        part = lax.dot_general(
            tokens_buffer[:, pl.ds(pl.multiple_of(f * depth, 128), depth)],
            slice_refs[j][:, :depth],
            (((1,), (1,)), ((), ())),
            preferred_element_type=jnp.float32,
        )
        low = part if low is None else low + part
    live = lax.broadcasted_iota(jnp.int32, (1, rank), 1) < rank_ref[...]
    low = jnp.where(live, low, 0.0).astype(jnp.bfloat16)
    low_ref[...] = low
    scale = ADAPTER_STRENGTH / rank_ref[...].astype(jnp.float32)
    update_ref[...] = scale * jnp.dot(
        low, up_ref[...], preferred_element_type=jnp.float32
    )


def low_and_update(z_n, place, live_rank, tokens, slices):
    rows, width = tokens.shape
    rank, slice_width = slices[0].shape
    depth = width // z_n
    up_width = slice_width - depth
    features = up_width * z_n
    smem = pl.BlockSpec(memory_space=pltpu.SMEM)
    vmem = pl.BlockSpec(memory_space=pltpu.VMEM)
    if depth % 128 == 0 and up_width % 128 == 0:
        return pl.pallas_call(
            functools.partial(low_kernel, z_n),
            in_specs=[smem, vmem, pl.BlockSpec(memory_space=pltpu.HBM)] + [vmem] * z_n,
            out_specs=[vmem] * 3,
            out_shape=[
                jax.ShapeDtypeStruct((rows, rank), jnp.bfloat16),
                jax.ShapeDtypeStruct((rank, features), jnp.bfloat16),
                jax.ShapeDtypeStruct((rows, features), jnp.float32),
            ],
            scratch_shapes=[pltpu.VMEM((rows, width), tokens.dtype), pltpu.SemaphoreType.DMA],
            compiler_params=pltpu.CompilerParams(vmem_limit_bytes=16 * 1024 * 1024),
        )(place, live_rank, tokens, *slices)
    z = place[0]
    stack = jnp.stack(slices)[(jnp.arange(z_n) - z) % z_n]
    down = jnp.swapaxes(stack[:, :, :depth], 0, 1).reshape(rank, width)
    up = jnp.swapaxes(stack[:, :, depth:], 0, 1).reshape(rank, features)
    low = lax.dot_general(
        tokens, down, (((1,), (1,)), ((), ())), preferred_element_type=jnp.float32
    )
    live = jnp.arange(rank, dtype=jnp.int32)[None, :] < live_rank
    low = jnp.where(live, low, 0.0).astype(jnp.bfloat16)
    scale = ADAPTER_STRENGTH / live_rank.astype(jnp.float32)
    return low, up, scale * jnp.dot(low, up, preferred_element_type=jnp.float32)


def norm_kernel(
    z_n, units, place_ref, columns_ref, rank_ref, *refs,
):
    base_refs, refs = refs[: 2 * units], refs[2 * units :]
    update_ref, low_ref, up_ref, cosine_ref, sine_ref, gain_ref = refs[:6]
    gradient_ref, tokens_ref, keys_ref = refs[6:9]
    refs = refs[9:]
    sent_refs, (tokens_buffer, gradient_buffer, part_up, semaphores) = refs[:-4], refs[-4:]
    fetch_gradient = pltpu.make_async_copy(gradient_ref, gradient_buffer, semaphores.at[0])
    fetch_tokens = pltpu.make_async_copy(tokens_ref, tokens_buffer, semaphores.at[1])
    fetch_gradient.start()
    fetch_tokens.start()
    z, core = place_ref[0], place_ref[1] % 2
    scale = ADAPTER_STRENGTH / rank_ref[...].astype(jnp.float32)
    head = gain_ref.shape[1]
    width = base_refs[0].shape[1]
    half = units * width
    low = low_ref[...]
    cosine, sine, gain = cosine_ref[...], sine_ref[...], gain_ref[...]
    gain_cosine, gain_sine = cosine * gain, sine * pltpu.roll(gain, head // 2, 1)
    grad_low = None
    fetch_gradient.wait()
    for n, base_ref in enumerate(base_refs):
        first = (core if n < units else 1 - core) * half + columns_ref[n % units]
        for i in range(width // head):
            at = pl.ds(pl.multiple_of(first + i * head, 128), head)
            up = up_ref[:, at]
            pre = base_ref[:, i * head : (i + 1) * head] + update_ref[:, at]
            inverse = lax.rsqrt(jnp.mean(pre * pre, axis=1, keepdims=True) + 1e-06)
            unit = pre * inverse
            keys = unit * gain_cosine + pltpu.roll(unit, head // 2, 1) * gain_sine
            keys_ref[:, at] = keys.astype(keys_ref.dtype)
            gradient = gradient_buffer[:, at].astype(jnp.float32)
            turned = gain * (gradient * cosine - pltpu.roll(gradient, head // 2, 1) * sine)
            along = jnp.mean(turned * unit, axis=1, keepdims=True)
            scaled = ((scale * inverse) * (turned - unit * along)).astype(jnp.bfloat16)
            part_low = lax.dot_general(
                scaled, up, (((1,), (1,)), ((), ())), preferred_element_type=jnp.float32
            )
            grad_low = part_low if grad_low is None else grad_low + part_low
            part_up[:, at] = lax.dot_general(
                low, scaled, (((0,), (0,)), ((), ())), preferred_element_type=jnp.float32
            ).astype(part_up.dtype)
    live = lax.broadcasted_iota(jnp.int32, (1, low.shape[1]), 1) < rank_ref[...]
    grad_low = jnp.where(live, grad_low, 0.0).astype(jnp.bfloat16)
    fetch_tokens.wait()
    if len(sent_refs) == 2:
        sent_refs[0][...] = lax.dot_general(
            grad_low, tokens_buffer[...], (((0,), (0,)), ((), ())),
            preferred_element_type=jnp.float32,
        ).astype(jnp.bfloat16)
        sent_refs[1][...] = part_up[...]
        return
    depth = tokens_ref.shape[1] // z_n
    up_width = part_up.shape[1] // z_n
    for j in range(z_n):
        f = (z + j) % z_n
        sent_refs[j][:, :depth] = lax.dot_general(
            grad_low,
            tokens_buffer[:, pl.ds(pl.multiple_of(f * depth, 128), depth)],
            (((0,), (0,)), ((), ())),
            preferred_element_type=jnp.float32,
        ).astype(jnp.bfloat16)
        sent_refs[j][:, depth:] = part_up[:, pl.ds(pl.multiple_of(f * up_width, 128), up_width)]


def norm_and_back(
    z_n, place, columns, live_rank, bases, update, low, up, cosine, sine, gain,
    gradient, tokens,
):
    rows, features = gradient.shape
    rank = up.shape[0]
    width = tokens.shape[1]
    depth, up_width = width // z_n, features // z_n
    aligned = depth % 128 == 0 and up_width % 128 == 0
    if aligned:
        sent = [jax.ShapeDtypeStruct((rank, depth + up_width), jnp.bfloat16)] * z_n
    else:
        sent = [
            jax.ShapeDtypeStruct((rank, width), jnp.bfloat16),
            jax.ShapeDtypeStruct((rank, features), jnp.bfloat16),
        ]
    smem = pl.BlockSpec(memory_space=pltpu.SMEM)
    vmem = pl.BlockSpec(memory_space=pltpu.VMEM)
    hbm = pl.BlockSpec(memory_space=pltpu.HBM)
    outs = pl.pallas_call(
        functools.partial(norm_kernel, z_n, len(bases) // 2),
        in_specs=[smem] * 2 + [vmem] * (len(bases) + 7) + [hbm] * 2,
        out_specs=[vmem] * (1 + len(sent)),
        out_shape=[jax.ShapeDtypeStruct((rows, features), jnp.bfloat16)] + sent,
        scratch_shapes=[
            pltpu.VMEM((rows, width), tokens.dtype),
            pltpu.VMEM((rows, features), gradient.dtype),
            pltpu.VMEM((rank, features), jnp.bfloat16),
            pltpu.SemaphoreType.DMA((2,)),
        ],
        compiler_params=pltpu.CompilerParams(vmem_limit_bytes=12 * 1024 * 1024),
    )(
        place, columns, live_rank, *bases, update, low, up, cosine, sine, gain,
        gradient, tokens,
    )
    if aligned:
        return outs[0], outs[1:]
    z = place[0]
    return outs[0], [
        jnp.concatenate(
            [
                lax.dynamic_slice(outs[1], (0, ((z + j) % z_n) * depth), (rank, depth)),
                lax.dynamic_slice(outs[2], (0, ((z + j) % z_n) * up_width), (rank, up_width)),
            ],
            axis=1,
        )
        for j in range(z_n)
    ]


def dots_kernel(z_n, shards, totals, packed, place_ref, tokens_ref, pair_ref, *refs):
    count = sum(len(group) for group in shards)
    unit_refs, refs = refs[:count], refs[count:]
    total_refs, out_refs = refs[:totals], refs[totals : totals + 2 * len(shards)]
    if packed:
        out_refs = [refs[totals].at[n] for n in range(2 * len(shards))]
    if totals == 1:
        total_refs = [total_refs[0].at[n] for n in range(2 * len(shards))]
    depth = unit_refs[0].shape[0]
    for side, ref in enumerate((tokens_ref, pair_ref)):
        n = 0
        for u, group in enumerate(shards):
            value = None
            for d in group:
                at = pl.multiple_of(((place_ref[0] - d + z_n) % z_n) * depth, 128)
                left = ref[:, pl.ds(at, depth)]
                part = jnp.dot(left, unit_refs[n][...], preferred_element_type=jnp.float32)
                value = part if value is None else value + part
                n += 1
            at = side * len(shards) + u
            if totals:
                value = total_refs[at][...] + (0.0 if value is None else value)
            out_refs[at][...] = value


def add_dots(z_n, place, tokens, pair, shards, units, totals, packed=False):
    rows = tokens.shape[0]
    depth, width = next(unit.shape for group in units for unit in group)
    count = len(shards)
    if depth % 128 or width % 128:
        outs = []
        for side, array in enumerate((tokens, pair)):
            for u, group in enumerate(shards):
                at = side * count + u
                value = 0.0 if not totals else totals[0][at] if len(totals) == 1 else totals[at]
                for d, unit in zip(group, units[u]):
                    at = ((place[0] - d) % z_n) * depth
                    value = value + jnp.dot(
                        lax.dynamic_slice(array, (0, at), (rows, depth)),
                        unit,
                        preferred_element_type=jnp.float32,
                    )
                outs.append(value)
        return [jnp.stack(outs)] if packed else outs
    vmem = pl.BlockSpec(memory_space=pltpu.VMEM)
    flat = [unit for group in units for unit in group]
    outs = pl.pallas_call(
        functools.partial(dots_kernel, z_n, shards, len(totals), packed),
        in_specs=[pl.BlockSpec(memory_space=pltpu.SMEM)] + [vmem] * (2 + len(flat) + len(totals)),
        out_specs=[vmem] * (1 if packed else 2 * count),
        out_shape=[jax.ShapeDtypeStruct((2 * count, rows, width), jnp.float32)]
        if packed
        else [jax.ShapeDtypeStruct((rows, width), jnp.float32)] * (2 * count),
        compiler_params=pltpu.CompilerParams(vmem_limit_bytes=20 * 1024 * 1024),
    )(place, tokens, pair, *flat, *totals)
    return list(outs)


def after(value, *others):
    return lax.optimization_barrier((value,) + others)[0]


def per_device(
    tokens,
    frozen_key_weight,
    key_norm_gain,
    adapter_down_weight,
    adapter_up_weight,
    packed_block_adapter,
    adapter_storage_row,
    live_adapter_rank,
    document_numbers,
    rotated_key_gradient,
):
    rows = tokens.shape[0]
    features = rotated_key_gradient.shape[1]
    depth = frozen_key_weight.shape[0]
    owned, rank, down_width = adapter_down_weight.shape
    up_width = adapter_up_weight.shape[2]
    copies_n = lax.axis_size("copies")
    z_n = lax.axis_size("fsdp")
    group_n = lax.axis_size("adapter")
    x_n = group_n // 2
    y = lax.axis_index("copies")
    z = lax.axis_index("fsdp")
    a = lax.axis_index("adapter")
    x, core = a // 2, a % 2

    def over_core(v):
        return lax.ppermute(v, "adapter", [(i, i ^ 1) for i in range(group_n)])

    def over_x(v, e):
        return lax.ppermute(
            v, "adapter", [(i, ((i // 2 + e) % x_n) * 2 + i % 2) for i in range(group_n)]
        )

    def over_y(v, g):
        return lax.ppermute(v, "copies", [(i, (i + g) % copies_n) for i in range(copies_n)])

    def over_z(v, d):
        return lax.ppermute(v, "fsdp", [(i, (i + d) % z_n) for i in range(z_n)])

    half = features // 2
    units = copies_n * x_n
    unit_width = half // units

    def unit_at(y_at, x_at):
        at = core * half + (y_at * x_n + x_at) * unit_width
        return lax.dynamic_slice(frozen_key_weight, (0, at), (depth, unit_width))

    unit = unit_at(y, x)
    sizes = (x_n, z_n)
    place = jnp.stack([z, a]).astype(jnp.int32)
    shifts = sorted(range(1, z_n), key=lambda d: min(d, z_n - d))
    final = len(shifts) - 1

    tokens_pair = over_core(tokens)
    picked = pick_rows(
        sizes, packed_block_adapter, adapter_storage_row, adapter_down_weight, adapter_up_weight
    )
    taken = [over_core(picked[x_n + e]) for e in range(x_n)]
    away = [picked[e] + after(taken[e], tokens_pair, taken[0]) for e in range(1, x_n)]
    slices = picked[0] + taken[0]
    from_z = {d: over_z(unit, d) for d in shifts[:2]}
    for d in shifts[2:]:
        step = 1 if 2 * d <= z_n else z_n - 1
        from_z[d] = over_z(after(from_z[(d - step) % z_n], *away), step)
    for e in range(1, x_n):
        slices = slices + over_x(away[e - 1], e)

    documents, packed, ranks, gain = lax.optimization_barrier(
        (
            document_numbers,
            packed_block_adapter,
            live_adapter_rank,
            key_norm_gain,
            away[0],
        )
    )[:4]
    mine = jnp.arange(packed.shape[0], dtype=jnp.int32) == z * group_n + a
    mine = jnp.arange(ranks.shape[0], dtype=jnp.int32) == jnp.sum(jnp.where(mine, packed, 0))
    live_rank = jnp.sum(jnp.where(mine, ranks, 0)).reshape(1, 1)
    cosine_part, sine_part = rope_tables(doc_positions(documents), key_norm_gain.shape[0])
    cosine = jnp.concatenate([cosine_part, cosine_part], axis=1)
    sine = jnp.concatenate([-sine_part, sine_part], axis=1)

    frozen_key_weight = after(frozen_key_weight, away[0])
    own_units = [
        unit_at((y - g) % copies_n, (x - e) % x_n) for g in range(copies_n) for e in range(x_n)
    ]
    totals = add_dots(
        z_n,
        after(place, cosine, sine, live_rank),
        tokens,
        tokens_pair,
        [[0]] * units,
        [[v] for v in own_units],
        [],
        packed=True,
    )
    along_x, along_y, diagonal = [], [], []
    for k, d in enumerate(shifts):
        gate = away[0] if k < 2 else along_y[k - 2][-1]
        along_y.append([over_y(after(from_z[d], gate), g) for g in range(1, copies_n)])
    for k, d in enumerate(shifts):
        gate = (along_y[0][-1], totals[0], along_y[1][-1])[min(k, 2)]
        along_x.append([over_x(after(from_z[d], gate), e) for e in range(1, x_n)])
    for k, d in enumerate(shifts):
        if k < final:
            gate = along_y[k + 1][-1]
            diagonal.append(
                [[over_y(after(v, gate), g) for v in along_x[k]] for g in range(1, copies_n)]
            )
    diagonal.append(
        [
            [over_x(after(v, along_x[max(final - 1, 0)][-1]), e) for e in range(1, x_n)]
            for v in along_y[final]
        ]
    )
    shards = {}
    for k, d in enumerate(shifts):
        shards[d] = [from_z[d]] + along_x[k]
        for g in range(1, copies_n):
            shards[d] += [along_y[k][g - 1]] + diagonal[k][g - 1]
    early, late = [], []
    for u in range(units):
        g, e = u // x_n, u % x_n
        early.append([d for d in shifts if not (g and e) and not (e and d == shifts[final])])
        late.append([d for d in shifts if d not in early[u]])
    totals = add_dots(
        z_n,
        place,
        tokens,
        tokens_pair,
        early,
        [[shards[d][u] for d in group] for u, group in enumerate(early)],
        totals,
    )
    adapter_slices = {0: slices[0]}
    for k, d in enumerate(shifts):
        gates = ()
        adapter_slices[(-d) % z_n] = over_z(after(slices[d], *gates), d)
    low, up, update = low_and_update(
        z_n,
        place,
        live_rank,
        tokens,
        [adapter_slices[j] for j in range(z_n)],
    )
    open_units = [u for u in range(units) if late[u]]
    done = add_dots(
        z_n,
        after(place, low),
        tokens,
        tokens_pair,
        [late[u] for u in open_units],
        [[shards[d][u] for d in late[u]] for u in open_units],
        [totals[u] for u in open_units] + [totals[units + u] for u in open_units],
    )
    bases = list(totals)
    for n, u in enumerate(open_units):
        bases[u], bases[units + u] = done[n], done[len(open_units) + n]
    bases = bases[:units] + [over_core(v) for v in bases[units:]]
    head = key_norm_gain.shape[0]
    columns = [
        (((y - g) % copies_n) * x_n + (x - e) % x_n) * unit_width
        for g in range(copies_n)
        for e in range(x_n)
    ]
    if unit_width % head:
        natural = []
        for side in (bases[:units], bases[units:]):
            stack = jnp.stack(side)
            order = jnp.stack(
                [
                    ((y - y_at) % copies_n) * x_n + (x - x_at) % x_n
                    for y_at in range(copies_n)
                    for x_at in range(x_n)
                ]
            )
            whole = jnp.swapaxes(stack[order], 0, 1).reshape(rows, half)
            natural.append(whole)
        bases = natural
        columns = [jnp.zeros_like(z)]

    rotated, sent = norm_and_back(
        z_n,
        place,
        jnp.stack(columns).astype(jnp.int32),
        live_rank,
        bases,
        update,
        low,
        up,
        cosine,
        sine,
        gain[None],
        rotated_key_gradient,
        tokens,
    )
    order = [0] + shifts if z_n <= 4 else list(range(z_n))
    step = -(-z_n // 4)
    groups = [tuple(order[k : k + step]) for k in range(0, z_n, step)]
    arrived = {d: sent[0] if d == 0 else over_z(sent[d], d) for d in order}
    blocks = []
    for group in groups:
        if len(group) == 1:
            here = arrived[group[0]][None]
        else:
            here = jnp.stack([arrived[d] for d in group])
        for e in range(x_n):
            there = over_x(here, e) if e else here
            blocks += [there, over_core(there)]
    grad_down, grad_up = owner_sum(
        sizes,
        groups,
        packed_block_adapter,
        adapter_storage_row,
        blocks,
        owned,
        down_width,
    )
    return (rotated, grad_down, grad_up)


def solution(mesh):
    return jax.shard_map(
        per_device,
        mesh=mesh,
        in_specs=(
            P(("copies", "fsdp", "adapter"), None),
            P("fsdp", None),
            P(),
            P("adapter", None, "fsdp"),
            P("adapter", None, "fsdp"),
            P("copies"),
            P(),
            P(),
            P(("copies", "fsdp", "adapter")),
            P(("copies", "fsdp", "adapter"), None),
        ),
        out_specs=(
            P(("copies", "fsdp", "adapter"), None),
            P(("copies", "adapter"), None, "fsdp"),
            P(("copies", "adapter"), None, "fsdp"),
        ),
        check_vma=False,
    )
```
